32 devices in a mesh: section: 2 (over core), dp: 16 (over z, y, x).
Axes of the slice: x: 2, y: 2, z: 4, core: 2. Of those that a mesh axis runs over, the one named last changes fastest.
Arguments:
- inputs: bfloat16 [16384, 1024], P('dp'), may hold values from -6 to 6
- qkv_weight: float32 [2, 1024, 3072], P('section', 'dp'), may hold values from -0.1875 to 0.1875
- out_weight: float32 [2, 1024, 1024], P('section', 'dp'), may hold values from -1.5 to 1.5
- cross_query: float32 [2, 1024, 1024], P('section', 'dp'), may hold values from -0.1875 to 0.1875
- cross_kv: float32 [2, 1024, 2048], P('section', 'dp'), may hold values from -0.1875 to 0.1875
- cross_out: float32 [2, 1024, 1024], P('section', 'dp'), may hold values from -1.5 to 1.5
- ffn_in: float32 [2, 1024, 4096], P('section', 'dp'), may hold values from -0.1875 to 0.1875
- ffn_out: float32 [2, 4096, 1024], P('section', 'dp'), may hold values from -0.21875 to 0.21875
- norm_gains: float32 [2, 3, 1024], P('section', None, 'dp'), may hold values from 0.1 to 1.9
- type_embed: float32 [2, 2, 1024], P('section', None, 'dp'), may hold values from -3 to 3
- encoder: bfloat16 [2, 16384, 1024], P('section', 'dp'), may hold values from -6 to 6
- lengths: int32 [32], P('dp'), may hold values from 128 to 512, as said below
- seq_types: int32 [32], P('dp'), may hold values from 0 to 1
- enc_mask: int32 [32, 512], P('dp'), may hold values from 0 to 1, as said below
- cotangent: bfloat16 [2, 16384, 1024], P('section', 'dp'), may hold values from -6 to 6
Outputs:
- layer_outputs: bfloat16 [2, 16384, 1024], P('section', 'dp')
- input_grads: bfloat16 [2, 16384, 1024], P('section', 'dp')
- encoder_grads: bfloat16 [2, 16384, 1024], P('section', 'dp')
- qkv_grad: float32 [2, 1024, 3072], P('section', 'dp')
- out_grad: float32 [2, 1024, 1024], P('section', 'dp')
- cross_query_grad: float32 [2, 1024, 1024], P('section', 'dp')
- cross_kv_grad: float32 [2, 1024, 2048], P('section', 'dp')
- cross_out_grad: float32 [2, 1024, 1024], P('section', 'dp')
- ffn_in_grad: float32 [2, 1024, 4096], P('section', 'dp')
- ffn_out_grad: float32 [2, 4096, 1024], P('section', 'dp')
- gains_grad: float32 [2, 3, 1024], P('section', None, 'dp')
- embed_grad: float32 [2, 2, 1024], P('section', None, 'dp')
The draws below stay inside these ranges and needn't reach their ends.
Inputs may be any that keep to these rules, and one draw needn't show every extreme that they name: `lengths`: some sequence has exactly 512 valid positions. `enc_mask`: each row is ones over its first frames and zeros after them, with at least 128 ones; some row is all ones.
All inputs are finite; a program needn't handle non-finite values.
Results may differ from the reference program's by a relative error of at most 0.018.
Values may be sent and summed in bfloat16 or wider, within the bound.
A program may use at most 768 MiB of HBM per device.

```python
import jax
import jax.numpy as jnp
from jax import lax

D = 1024
HEADS = 16
HEAD_DIM = 64
FF = 4096
LEN = 512
ENC = 512
SEQS = 32
TOKENS = 16384
FRAMES = 16384


def draw_lengths(key, part):
    key = jax.random.fold_in(key, 11)
    first, second = jax.random.split(key)
    values = jax.random.randint(first, (SEQS,), LEN // 4, LEN + 1)
    chosen = jax.random.randint(second, (), 0, SEQS)
    return jnp.where(jnp.arange(SEQS) == chosen, LEN, values).astype(jnp.int32)


def draw_enc_mask(key, part):
    key = jax.random.fold_in(key, 23)
    first, second = jax.random.split(key)
    valid = jax.random.randint(first, (SEQS,), ENC // 4, ENC + 1)
    chosen = jax.random.randint(second, (), 0, SEQS)
    valid = jnp.where(jnp.arange(SEQS) == chosen, ENC, valid)
    return (jnp.arange(ENC)[None, :] < valid[:, None]).astype(jnp.int32)


def with_ends(entries, own_key, low, largest):
    longest = entries.shape.index(max(entries.shape))
    spots = []
    for shift in (0, 1):
        where = [jax.random.randint(jax.random.fold_in(own_key, axis), (), 0, length) for axis, length in enumerate(entries.shape)]
        where[longest] = (where[longest] + shift) % entries.shape[longest]
        spots.append(tuple(where))
    return entries.at[spots[0]].set(low).at[spots[1]].set(largest)


def block_scale(key, dims, cuts, smallest, high):
    level = 1.0
    for dim, parts in cuts:
        heights = jax.random.uniform(jax.random.fold_in(jax.random.fold_in(key, 6), dim), (parts,), jnp.float32, smallest / len(cuts), high / len(cuts))
        level = level * jnp.repeat(jnp.exp(heights), dims[dim] // parts).reshape((-1,) + (1,) * (len(dims) - 1 - dim))
    return level


def noise(rng, dims, spread, reach, cuts=(), kind=jnp.bfloat16):
    result = jax.random.normal(rng, dims, jnp.float32) * spread
    if len(cuts) > 0:
        result = block_scale(rng, dims, cuts, -0.22, 0.18) * result
    return jnp.clip(result, min=-reach, max=reach).astype(kind)


def setup_inputs(seed: int = 0) -> dict:
    arg_keys = jax.random.split(jax.random.key(seed), 16)
    return {
        "inputs": noise(arg_keys[0], (TOKENS, D), 1.0, 6.0, ((0, 16),)),
        "qkv_weight": noise(arg_keys[1], (2, D, 3 * D), D ** -0.5, 0.1875, ((0, 2), (1, 16)), jnp.float32),
        "out_weight": noise(arg_keys[2], (2, D, D), (max(D // 64, 4)) ** -0.5, 1.5, ((0, 2), (1, 16)), jnp.float32),
        "cross_query": noise(arg_keys[3], (2, D, D), D ** -0.5, 0.1875, ((0, 2), (1, 16)), jnp.float32),
        "cross_kv": noise(arg_keys[4], (2, D, 2 * D), D ** -0.5, 0.1875, ((0, 2), (1, 16)), jnp.float32),
        "cross_out": noise(arg_keys[5], (2, D, D), (max(D // 64, 4)) ** -0.5, 1.5, ((0, 2), (1, 16)), jnp.float32),
        "ffn_in": noise(arg_keys[6], (2, D, FF), D ** -0.5, 0.1875, ((0, 2), (1, 16)), jnp.float32),
        "ffn_out": noise(arg_keys[7], (2, FF, D), (FF // 6) ** -0.5, 0.21875, ((0, 2), (1, 16)), jnp.float32),
        "norm_gains": jnp.clip(1.0 + 0.18 * jax.random.normal(arg_keys[8], (2, 3, D), jnp.float32), 0.1, 1.9),
        "type_embed": noise(arg_keys[9], (2, 2, D), 0.5, 3.0, ((0, 2), (2, 16)), jnp.float32),
        "encoder": noise(arg_keys[10], (2, FRAMES, D), 1.0, 6.0, ((0, 2), (1, 16))),
        "lengths": draw_lengths(jax.random.fold_in(arg_keys[15], 71), 0),
        "seq_types": with_ends(jax.random.randint(arg_keys[12], (SEQS,), 0, 2), jax.random.fold_in(arg_keys[12], 1), 0, 1).astype(jnp.int32),
        "enc_mask": draw_enc_mask(jax.random.fold_in(arg_keys[15], 71), 0),
        "cotangent": noise(arg_keys[14], (2, TOKENS, D), 1.0, 6.0, ((0, 2), (1, 16))),
    }


@jax.custom_vjp
def low(v):
    return lax.optimization_barrier(v.astype(jnp.bfloat16)).astype(jnp.float32)

@jax.custom_vjp
def low_back(v):
    return v

def low_keep(v):
    return (low(v), None)

def low_pass(kept, grad):
    return (grad,)

def back_keep(v):
    return (v, None)

def back_low(kept, grad):
    return (low(grad),)
low.defvjp(low_keep, low_pass)
low_back.defvjp(back_keep, back_low)
EPS = 1e-05
HIGH = lax.Precision.HIGHEST

def both(v):
    return low(low_back(v))

def mat(a, b):
    return jnp.dot(a, b, precision=HIGH)

def norm_rows(h, gain):
    mean = lax.optimization_barrier(jnp.mean(h, -1, keepdims=True))
    cent = h - mean
    var = lax.optimization_barrier(jnp.mean(cent * cent, -1, keepdims=True))
    return cent * lax.rsqrt(var + EPS) * gain

def attend(query, keys, values, allow):
    rows = query.shape[0]
    cols = keys.shape[0]
    query_h = query.reshape(rows, HEADS, HEAD_DIM)
    keys_h = keys.reshape(cols, HEADS, HEAD_DIM)
    values_h = values.reshape(cols, HEADS, HEAD_DIM)
    scores = jnp.einsum('qhd,khd->hqk', query_h, keys_h, precision=HIGH) * HEAD_DIM ** (-0.5)
    scores = low_back(jnp.where(allow[None], scores, -1e+30))
    top = lax.optimization_barrier(jnp.max(scores, -1, keepdims=True))
    expo = jnp.exp(scores - top)
    probs = low(expo / lax.optimization_barrier(jnp.sum(expo, -1, keepdims=True)))
    out = jnp.einsum('hqk,khd->qhd', probs, values_h, precision=HIGH)
    return out.reshape(rows, HEADS * HEAD_DIM)

def layer(h, weights, memory, lengths, seq_types, enc_mask):
    qkv_w, out_w, cq_w, ckv_w, cout_w, fin_w, fout_w, gains, embed = [low(w) for w in weights]
    type_rows = jnp.repeat(seq_types, LEN)
    start = h + jnp.where((type_rows == 1)[:, None], embed[1], embed[0])
    qkv = both(mat(low(norm_rows(start, gains[0])), qkv_w))

    def self_one(args):
        block, length = args
        position = jnp.arange(LEN)
        allow = (position[None, :] <= position[:, None]) & (position[None, :] < length)
        return attend(block[:, :D], block[:, D:2 * D], block[:, 2 * D:], allow)
    ctx = both(lax.map(jax.checkpoint(self_one), (qkv.reshape(SEQS, LEN, 3 * D), lengths)).reshape(TOKENS, D))
    mid = start + low_back(mat(ctx, out_w))
    cross_q = both(mat(low(norm_rows(mid, gains[1])), cq_w))
    cross_mem = both(mat(memory, ckv_w))

    def cross_one(args):
        query, kept, mask_row = args
        allow = jnp.broadcast_to(mask_row[None, :] == 1, (LEN, ENC))
        return attend(query, kept[:, :D], kept[:, D:], allow)
    ctx_cross = both(lax.map(jax.checkpoint(cross_one), (cross_q.reshape(SEQS, LEN, D), cross_mem.reshape(SEQS, ENC, 2 * D), enc_mask)).reshape(TOKENS, D))
    late = mid + low_back(mat(ctx_cross, cout_w))
    up = low_back(mat(low(norm_rows(late, gains[2])), fin_w))
    act = low(jax.nn.gelu(up, approximate=False))
    return late + low_back(mat(act, fout_w))

def forward(inputs, shift, weights, memory, lengths, seq_types, enc_mask):
    first = layer(inputs, tuple((w[0] for w in weights)), memory[0], lengths, seq_types, enc_mask)
    second_in = low_back(low(first)) + shift
    second = layer(second_in, tuple((w[1] for w in weights)), memory[1], lengths, seq_types, enc_mask)
    return jnp.stack([first, second])

def reference(inputs, qkv_weight, out_weight, cross_query, cross_kv, cross_out, ffn_in, ffn_out, norm_gains, type_embed, encoder, lengths, seq_types, enc_mask, cotangent):
    weights = (qkv_weight, out_weight, cross_query, cross_kv, cross_out, ffn_in, ffn_out, norm_gains, type_embed)
    start = inputs.astype(jnp.float32)
    memory = encoder.astype(jnp.float32)
    shift = jnp.zeros_like(start)

    def whole(a, b, c, d):
        return forward(a, b, c, d, lengths, seq_types, enc_mask)
    outs, pull = jax.vjp(whole, start, shift, weights, memory)
    d_start, d_shift, d_weights, d_memory = pull(cotangent.astype(jnp.float32))
    return (outs.astype(jnp.bfloat16), jnp.stack([d_start, d_shift]).astype(jnp.bfloat16), d_memory.astype(jnp.bfloat16), d_weights[0], d_weights[1], d_weights[2], d_weights[3], d_weights[4], d_weights[5], d_weights[6], d_weights[7], d_weights[8])
```

```python
import functools

import jax
import jax.numpy as jnp
from jax import lax
from jax.experimental import pallas as pl
from jax.experimental.pallas import tpu as pltpu
from jax.sharding import PartitionSpec as P

D = 1024
HEADS = 16
SEQ = 512
EPS = 1e-05
NEG = -1e30
MESH = pl.DeviceIdType.MESH
HALF = jnp.bfloat16
FULL = jnp.float32
TILE = 256
ROWS = 64


def grid_of(n):
    deep = 4 if n % 4 == 0 else 1
    rest = n // deep
    wide = max(k for k in range(1, rest + 1) if rest % k == 0 and k * k <= rest)
    return (deep, wide, rest // wide)


class Place:
    def __init__(self, dims):
        self.dims = dims
        self.chip = lax.axis_index("dp")
        self.core = lax.axis_index("section")
        self.other = 1 - self.core
        deep, wide, long = dims
        self.at = (
            self.chip // (wide * long),
            lax.rem(self.chip // long, wide),
            lax.rem(self.chip, long),
        )

    def shifted(self, axis, step):
        where = list(self.at)
        where[axis] = lax.rem(self.at[axis] + step + self.dims[axis], self.dims[axis])
        return where

    def peer(self, axis, step):
        where = self.shifted(axis, step)
        return (self.core, (where[0] * self.dims[1] + where[1]) * self.dims[2] + where[2])

    def twin(self):
        return (self.other, self.chip)

    def greet(self):
        barrier = pltpu.get_barrier_semaphore()
        peers = [self.peer(a, s) for a in range(3) for s in range(1, self.dims[a])]
        peers.append(self.twin())
        for peer in peers:
            pl.semaphore_signal(barrier, inc=1, device_id=peer, device_id_type=MESH)
        pl.semaphore_wait(barrier, len(peers))


def remote(src, dst, send, recv, peer):
    return pltpu.make_async_remote_copy(
        src_ref=src, dst_ref=dst, send_sem=send, recv_sem=recv, device_id=peer, device_id_type=MESH
    )


def local(src, dst, sem):
    return pltpu.make_async_copy(src, dst, sem)


def nt_dot(left, right):
    return lax.dot_general(
        left, right, (((1,), (1,)), ((), ())), preferred_element_type=FULL
    )


def nn_dot(left, right):
    return jnp.dot(left, right, preferred_element_type=FULL)


def tile(i, size=TILE):
    return pl.ds(pl.multiple_of(i * size, size), size)


def loop(count, body):
    def step(i, carry):
        body(i)
        return carry

    lax.fori_loop(0, count, step, 0)


def lane_half(a):
    lane = lax.broadcasted_iota(jnp.int32, (1, 128), 1)
    return jnp.where((lane // 64) == a, 1.0, 0.0).astype(HALF)


def allowed(keys, first, count, causal):
    key = lax.broadcasted_iota(jnp.int32, (keys, TILE), 0)
    ok = key < count
    if causal:
        ok = ok & (key <= first + lax.broadcasted_iota(jnp.int32, (keys, TILE), 1))
    return ok


ORDER_A = (0, 2, 1)
ORDER_B = (0, 1, 2)


def forward_kernel(
    dims,
    meta,
    pack,
    small,
    hidden,
    frames,
    w_all,
    y_out,
    six_out,
    xt_out,
    actt_out,
    dg_out,
    xh_out,
    rstd_out,
    lse_out,
    vec_out,
    ws,
    res,
    xb,
    mem,
    six,
    xt,
    actn,
    actt,
    dg,
    xh,
    hin,
    yb,
    vecs,
    seed_sem,
    swap_send,
    swap_recv,
    hop_send,
    hop_recv,
    twin_send,
    twin_recv,
    vec_send,
    vec_recv,
    vec_swap,
    in_sem,
    frame_sem,
    y_sem,
    w_sem,
    save_sem,
):
    place = Place(dims)
    core, other, at = place.core, place.other, place.at
    place.greet()

    def seed(g):
        return local(
            pack.at[g, pl.ds(2 * core, 2)],
            w_all.at[pl.ds((core * 4 + g) * 4 + 2 * core, 2), at[0], at[1], at[2]],
            seed_sem.at[g],
        )

    def swap(g):
        return remote(
            pack.at[g, pl.ds(2 * other, 2)],
            w_all.at[pl.ds((core * 4 + g) * 4 + 2 * other, 2), at[0], at[1], at[2]],
            swap_send.at[g],
            swap_recv.at[g],
            place.twin(),
        )

    def swapped(layer, g):
        spot = w_all.at[pl.ds((layer * 4 + g) * 4 + 2 * core, 2), at[0], at[1], at[2]]
        return remote(spot, spot, swap_send.at[g], swap_recv.at[g], place.twin())

    own_vec = vecs.at[core, at[0], at[1], at[2]]
    vec_in = local(small, own_vec, in_sem.at[0])
    vec_in.start()
    mine = pl.ds(core * SEQ, SEQ)
    twins = pl.ds(other * SEQ, SEQ)
    hid_in = local(hidden.at[mine], hin, in_sem.at[1])
    hid_in.start()
    mem_in = local(frames.at[mine], mem.at[core], in_sem.at[2])
    mem_in.start()
    for g in range(4):
        seed(g).start()
        swap(g).start()
    mem_swap = remote(
        frames.at[twins], mem.at[core], frame_sem.at[0], frame_sem.at[1], place.twin()
    )
    mem_swap.start()

    orders = [ORDER_A, ORDER_B] * 8

    def block_of(u):
        return (u // 2) * 4 + 2 * core + u % 2

    def part(order, k, shift):
        index = []
        for axis in range(3):
            if axis in order[:k]:
                index.append(slice(None))
            elif axis == order[k]:
                index.append(place.shifted(axis, -shift)[axis])
            else:
                index.append(at[axis])
        return tuple(index)

    def hop(u, k, step):
        here = w_all.at[(block_of(u),) + part(orders[u], k, 0)]
        return remote(
            here,
            here,
            hop_send.at[u, k, step - 1],
            hop_recv.at[u, k, step - 1],
            place.peer(orders[u][k], step),
        )

    def hop_arrival(u, k, step):
        there = w_all.at[(block_of(u),) + part(orders[u], k, step)]
        return remote(
            there, there, hop_send.at[u, k, step - 1], hop_recv.at[u, k, step - 1], place.twin()
        )

    def twin_copy(u, block):
        return remote(
            w_all.at[block], w_all.at[block], twin_send.at[u], twin_recv.at[u], place.twin()
        )

    def vec_hop(k, step):
        here = vecs.at[(core,) + part(ORDER_B, k, 0)]
        return remote(
            here, here, vec_send.at[k, step - 1], vec_recv.at[k, step - 1],
            place.peer(ORDER_B[k], step),
        )

    def vec_arrival(k, step):
        there = vecs.at[(core,) + part(ORDER_B, k, step)]
        return remote(
            there, there, vec_send.at[k, step - 1], vec_recv.at[k, step - 1], place.twin()
        )

    def vec_twin(layer):
        return remote(
            vecs.at[layer], vecs.at[layer], vec_swap.at[0], vec_swap.at[1], place.twin()
        )

    def vec_event(k):
        if k == 0:
            vec_in.wait()
        if 0 < k <= 3:
            for step in range(1, dims[ORDER_B[k - 1]]):
                vec_arrival(k - 1, step).wait_recv()
        if k < 3:
            for step in range(1, dims[ORDER_B[k]]):
                vec_hop(k, step).start()
        elif k == 3:
            vec_twin(core).start()
        else:
            vec_twin(other).wait_recv()

    def event(u, k):
        layer, g = u // 8, (u // 2) % 4
        if k == 0 and u % 2 == 0:

            @pl.when(core == layer)
            def _():
                seed(g).wait()

            @pl.when(core != layer)
            def _():
                swapped(layer, g).wait_recv()

        if 0 < k <= 3:
            for step in range(1, dims[orders[u][k - 1]]):
                hop_arrival(u, k - 1, step).wait_recv()
        if k < 3:
            for step in range(1, dims[orders[u][k]]):
                hop(u, k, step).start()
        elif k == 3:
            twin_copy(u, block_of(u)).start()
        else:
            twin_copy(u, (u // 2) * 4 + 2 * other + u % 2).wait_recv()

    def service(t):
        for k in (4, 3, 2, 1, 0):
            if t == k:
                vec_event(k)
            s = t - k
            if 0 <= s < 8:
                event(2 * s, k)
                event(2 * s + 1, k)

    def save_to(layer, kind, i):
        src, dst, first = {
            "six": (six, six_out, 0),
            "xt": (xt, xt_out, 6),
            "actt": (actt, actt_out, 12),
            "dg": (dg, dg_out, 16),
            "xh": (xh, xh_out, 20),
        }[kind]
        return local(src.at[i], dst.at[layer, i], save_sem.at[first + i])

    saves = (
        [("six", i) for i in range(6)]
        + [("xt", i) for i in range(6)]
        + [("actt", i) for i in range(4)]
        + [("dg", i) for i in range(4)]
        + [("xh", i) for i in range(3)]
    )

    def weight(s, n):
        return ws[s, :, :, :, :, tile(n)].reshape(D, TILE)

    for t in range(4):
        service(t)
    hid_in.wait()
    mem_in.wait()
    remote(
        frames.at[mine], mem.at[other], frame_sem.at[0], frame_sem.at[1], place.twin()
    ).wait_recv()

    count_self = meta[0, core]
    kind = meta[1, core]
    count_cross = meta[2, core]

    def layer_body(l):
        def guard(what, i):
            @pl.when(l > 0)
            def _():
                save_to(l - 1, what, i).wait()

        def save(what, i):
            save_to(l, what, i).start()

        def fetch(g):
            @pl.when(l == 0)
            def _():
                service(g + 4)

            @pl.when(l == 1)
            def _():
                service(g + 8)

            for q in range(4):
                local(w_all.at[(l * 4 + g) * 4 + q], ws.at[q], w_sem.at[q]).start()

        def ready(g, q):
            local(w_all.at[(l * 4 + g) * 4 + q], ws.at[q], w_sem.at[q]).wait()

        def flip(src, i):
            guard("xt", i)

            def step(n):
                xt[i, tile(n), :] = src[:, tile(n)].T

            loop(D // TILE, step)
            save("xt", i)

        def norm(j):
            gain = vec_out[l, pl.ds(j, 1), :]
            guard("xh", j)

            def step(i):
                rows = tile(i, ROWS)
                v = res[rows, :]
                cent = v - jnp.mean(v, -1, keepdims=True)
                rstd = lax.rsqrt(jnp.mean(cent * cent, -1, keepdims=True) + EPS)
                hat = cent * rstd
                xh[j, rows, :] = hat
                rstd_out[l, j, rows, :] = jnp.broadcast_to(rstd, (ROWS, 128))
                xb[rows, :] = (hat * gain).astype(HALF)

            loop(SEQ // ROWS, step)
            save("xh", j)

        def project(src, s, i):
            guard("six", i)

            def step(n):
                six[i, :, tile(n)] = nn_dot(src[...], weight(s, n)).astype(HALF)

            loop(D // TILE, step)
            save("six", i)

        def attend(qi, ki, vi, which, out, count, causal):
            guard("xt", out)

            def pair(hp):
                cols = tile(hp, 128)
                q2 = six[qi, :, cols] * jnp.asarray(0.125, HALF)
                k2 = six[ki, :, cols]
                vt = six[vi, :, cols].T
                for a in range(2):
                    ka = k2 * lane_half(a)
                    for first in range(0, SEQ, TILE):
                        keys = first + TILE if causal else SEQ
                        s = nt_dot(ka[:keys], q2[first : first + TILE])
                        s = jnp.where(allowed(keys, first, count, causal), s, NEG)
                        top = jnp.max(s, 0, keepdims=True)
                        expo = jnp.exp(s - top)
                        total = jnp.sum(expo, 0, keepdims=True)
                        p = (expo * (1.0 / total)).astype(HALF)
                        o = nn_dot(vt[a * 64 : a * 64 + 64, :keys], p)
                        xt[out, pl.ds(hp * 128 + a * 64, 64), pl.ds(first, TILE)] = o.astype(HALF)
                        lse_out[l, which, hp, pl.ds(a, 1), pl.ds(first, TILE)] = top + jnp.log(
                            total
                        )
                xb[:, cols] = xt[out, tile(hp, 128), :].T

            loop(HEADS // 2, pair)
            save("xt", out)

        def add_product(src, s):
            def step(n):
                res[:, tile(n)] += nn_dot(src[...], weight(s, n))

            loop(D // TILE, step)

        fetch(0)

        @pl.when(l == 0)
        def _():
            rank = D // (dims[0] * dims[1] * dims[2])
            vec_out[...] = jnp.zeros(vec_out.shape, FULL)

            def step(j):
                row = lax.broadcasted_iota(jnp.int32, (128, D), 0)
                col = lax.broadcasted_iota(jnp.int32, (128, D), 1)
                spread = jnp.where((col == j * rank + row) & (row < rank), 1.0, 0.0).astype(HALF)
                z = j // (dims[1] * dims[2])
                y = lax.rem(j // dims[2], dims[1])
                x = lax.rem(j, dims[2])
                for m in range(2):
                    vec_out[m] += nn_dot(vecs[m, z, y, x], spread)

            loop(dims[0] * dims[1] * dims[2], step)

        shift = jnp.where(kind == 1, vec_out[l, pl.ds(4, 1), :], vec_out[l, pl.ds(3, 1), :])

        def begin(i):
            rows = tile(i, ROWS)
            came = jnp.where(l == 0, hin[rows, :].astype(FULL), yb[0, rows, :].astype(FULL))
            res[rows, :] = came + shift

        loop(SEQ // ROWS, begin)
        norm(0)
        flip(xb, 0)
        for q in range(3):
            ready(0, q)
            project(xb, q, q)
        attend(0, 1, 2, 0, 1, count_self, True)
        ready(0, 3)
        add_product(xb, 3)
        norm(1)
        flip(xb, 3)
        fetch(1)
        ready(1, 2)
        project(xb, 2, 3)
        flip(mem.at[l], 2)
        ready(1, 0)
        project(mem.at[l], 0, 4)
        ready(1, 1)
        project(mem.at[l], 1, 5)
        attend(3, 4, 5, 1, 4, count_cross, False)
        ready(1, 3)
        add_product(xb, 3)
        norm(2)
        flip(xb, 5)
        fetch(2)
        for q in range(4):
            ready(2, q)
            guard("dg", q)
            guard("actt", q)

            def up(n, q=q):
                u = nn_dot(xb[...], weight(q, n))
                cdf = 0.5 * (1.0 + lax.erf(u * (0.5**0.5)))
                act = (u * cdf).astype(HALF)
                actn[q, :, tile(n)] = act
                actt[q, tile(n), :] = act.T
                bell = jnp.exp(-0.5 * u * u) * 0.3989422804014327
                dg[q, :, tile(n)] = (cdf + u * bell).astype(HALF)

            loop(D // TILE, up)
            save("dg", q)
            save("actt", q)
        fetch(3)
        for q in range(4):
            ready(3, q)

        def down(n):
            total = res[:, tile(n)]
            for q in range(4):
                total += nn_dot(actn[q], weight(q, n))
            yb[l, :, tile(n)] = total.astype(HALF)

        loop(D // TILE, down)

        @pl.when(core == l)
        def _():
            local(yb.at[l], y_out.at[mine], y_sem.at[0]).start()

        @pl.when(core != l)
        def _():
            remote(yb.at[l], y_out.at[mine], y_sem.at[1], y_sem.at[2], place.twin()).start()

    loop(2, layer_body)

    for what, i in saves:
        save_to(1, what, i).wait()
    local(yb.at[core], y_out.at[mine], y_sem.at[0]).wait()
    remote(yb.at[other], y_out.at[mine], y_sem.at[1], y_sem.at[2], place.twin()).wait_send()
    remote(yb.at[core], y_out.at[twins], y_sem.at[1], y_sem.at[2], place.twin()).wait_recv()
    mem_swap.wait_send()
    for g in range(4):
        swap(g).wait_send()
    for k in range(3):
        for step in range(1, dims[ORDER_B[k]]):
            vec_hop(k, step).wait_send()
    vec_twin(core).wait_send()
    for u in range(16):
        for k in range(3):
            for step in range(1, dims[orders[u][k]]):
                hop(u, k, step).wait_send()
        twin_copy(u, block_of(u)).wait_send()


def run_forward(dims, meta, pack, small, hidden, frames):
    rank = D // (dims[0] * dims[1] * dims[2])
    anyw = pl.BlockSpec(memory_space=pl.ANY)
    vmem = pl.BlockSpec(memory_space=pltpu.VMEM)
    hops = max(dims) - 1
    dma = pltpu.SemaphoreType.DMA
    shape = jax.ShapeDtypeStruct
    return pl.pallas_call(
        functools.partial(forward_kernel, dims),
        out_shape=(
            shape((32,) + dims + (rank, D), HALF),
            shape((2 * SEQ, D), HALF),
            shape((2, 6, SEQ, D), HALF),
            shape((2, 6, D, SEQ), HALF),
            shape((2, 4, D, SEQ), HALF),
            shape((2, 4, SEQ, D), HALF),
            shape((2, 3, SEQ, D), FULL),
            shape((2, 3, SEQ, 128), FULL),
            shape((2, 2, HEADS // 2, 2, SEQ), FULL),
            shape((2, 16, D), FULL),
        ),
        in_specs=[pl.BlockSpec(memory_space=pltpu.SMEM)] + [anyw] * 4,
        out_specs=(anyw,) * 7 + (vmem,) * 3,
        scratch_shapes=[
            pltpu.VMEM((4,) + dims + (rank, D), HALF),
            pltpu.VMEM((SEQ, D), FULL),
            pltpu.VMEM((SEQ, D), HALF),
            pltpu.VMEM((2, SEQ, D), HALF),
            pltpu.VMEM((6, SEQ, D), HALF),
            pltpu.VMEM((6, D, SEQ), HALF),
            pltpu.VMEM((4, SEQ, D), HALF),
            pltpu.VMEM((4, D, SEQ), HALF),
            pltpu.VMEM((4, SEQ, D), HALF),
            pltpu.VMEM((3, SEQ, D), FULL),
            pltpu.VMEM((SEQ, D), HALF),
            pltpu.VMEM((2, SEQ, D), HALF),
            pltpu.VMEM((2,) + dims + (16, 128), HALF),
            dma((4,)),
            dma((4,)),
            dma((4,)),
            dma((16, 3, hops)),
            dma((16, 3, hops)),
            dma((16,)),
            dma((16,)),
            dma((3, hops)),
            dma((3, hops)),
            dma((2,)),
            dma((3,)),
            dma((2,)),
            dma((3,)),
            dma((4,)),
            dma((23,)),
        ],
        compiler_params=pltpu.CompilerParams(
            collective_id=0, has_side_effects=True, vmem_limit_bytes=60 * 2**20
        ),
        cost_estimate=pl.CostEstimate(
            flops=40 * 10**9, bytes_accessed=3 * 10**8, transcendentals=10**7
        ),
    )(meta, pack, small, hidden, frames)


def packed(qkv_weight, out_weight, cross_query, cross_kv, cross_out, ffn_in, ffn_out, chips):
    rank = qkv_weight.shape[1]

    def columns(w):
        return jnp.moveaxis(w[0].astype(HALF).reshape(rank, -1, D), 1, 0)

    inner = ffn_in[0].astype(HALF).reshape(rank, chips, 4, rank)
    inner = inner.transpose(2, 0, 1, 3).reshape(4, rank, D)
    outer = ffn_out[0].astype(HALF).reshape(4, rank, D)
    first = jnp.concatenate([columns(qkv_weight), columns(out_weight)], 0)
    second = jnp.concatenate([columns(cross_kv), columns(cross_query), columns(cross_out)], 0)
    return jnp.stack([first, second, inner, outer])


def small_block(norm_gains, type_embed):
    rows = jnp.concatenate([norm_gains[0], type_embed[0]], 0).astype(HALF)
    return jnp.pad(rows, ((0, 16 - rows.shape[0]), (0, 128 - rows.shape[1])))


RS_EVEN = (1, 2, 0)
RS_ODD = (2, 1, 0)
LAGS = (1, 2, 3, 4)
SLOTS = 8
PAIRS = ((12, 8), (13, 9), (14, 10), (15, 11), (4, 5), (7, 6), (3, 0), (1, 2))


def backward_kernel(
    dims,
    meta,
    cot,
    w_all,
    six_in,
    xt_in,
    actt_in,
    dg_in,
    xh_in,
    rstd,
    lse,
    vec,
    dx_out,
    de_out,
    grad_out,
    small_out,
    cot_land,
    land_s,
    land_0,
    land_1,
    land_2,
    stage,
    ws,
    g,
    dx,
    gb,
    qkv,
    work,
    xtb,
    xh,
    tmp_s,
    tmp_0,
    tmp_1,
    tmp_2,
    dxb,
    deb,
    fin,
    sm,
    sm_land,
    w_sem,
    six_sem,
    xt_sem,
    dg_sem,
    xh_sem,
    cot_sem,
    cot_swap,
    s_send,
    s_recv,
    hop_send,
    hop_recv,
    tmp_sem,
    fin_sem,
    fin_send,
    fin_recv,
    out_sem,
    small_send,
    small_recv,
):
    place = Place(dims)
    core, other, at = place.core, place.other, place.at
    rank = D // (dims[0] * dims[1] * dims[2])
    chunk = D // dims[0]
    place.greet()
    mine = pl.ds(core * SEQ, SEQ)
    twins = pl.ds(other * SEQ, SEQ)
    cot_send = remote(cot.at[twins], cot_land, cot_swap.at[0], cot_swap.at[1], place.twin())
    cot_send.start()
    kind = meta[1, core]

    def load_w(slot, layer, b):
        return local(w_all.at[layer * 16 + b], ws.at[slot], w_sem.at[slot])

    def load_six(slot, layer, i):
        return local(six_in.at[layer, i], qkv.at[slot], six_sem.at[slot])

    def load_xt(slot, layer, i):
        return local(xt_in.at[layer, i], xtb.at[slot], xt_sem.at[slot])

    def load_act(slot, layer, q):
        return local(actt_in.at[layer, q], xtb.at[slot], xt_sem.at[slot])

    def load_dg(slot, layer, q):
        return local(dg_in.at[layer, q], work.at[slot], dg_sem.at[slot])

    def load_xh(layer, j):
        return local(xh_in.at[layer, j], xh, xh_sem.at[0])

    def order_of(parity):
        return RS_EVEN if parity == 0 else RS_ODD

    def widest(order):
        return dims[order[1]]

    def region(order, k, step):
        index = []
        for axis in range(3):
            if axis in order[:k]:
                index.append(at[axis])
            elif axis == order[k]:
                index.append(place.shifted(axis, step)[axis])
            else:
                index.append(slice(None))
        return tuple(index)

    def landing(order, k, u, step):
        if k == 0:
            return land_0.at[u, step - 1, :, pl.ds(0, widest(order))]
        if k == 1:
            return land_1.at[u, step - 1]
        return land_2.at[u, step - 1]

    def hop(u, slot, parity, k, step):
        order = order_of(parity)
        return remote(
            stage.at[(slot,) + region(order, k, step)],
            landing(order, k, u, step),
            hop_send.at[u, k, step - 1],
            hop_recv.at[u, k, step - 1],
            place.peer(order[k], step),
        )

    def steps(parity, k):
        return range(1, dims[order_of(parity)[k]])

    def tmp_load(k, u, parity):
        order = order_of(parity)
        if k == 0:
            return [local(land_s.at[u], tmp_s, tmp_sem.at[0, 0])]
        pairs = []
        for step in steps(parity, k - 1):
            if k == 1:
                dst = tmp_0.at[step - 1, :, pl.ds(0, widest(order))]
            elif k == 2:
                dst = tmp_1.at[step - 1]
            else:
                dst = tmp_2.at[step - 1]
            pairs.append(local(landing(order, k - 1, u, step), dst, tmp_sem.at[k, step - 1]))
        return pairs

    def sib_send(u, parity):
        return remote(
            stage.at[SLOTS + parity], land_s.at[u], s_send.at[u], s_recv.at[u], place.twin()
        )

    def own_block(j):
        return jnp.where(core == 0, PAIRS[j][0], PAIRS[j][1])

    def twin_block(j):
        return jnp.where(core == 0, PAIRS[j][1], PAIRS[j][0])

    def fin_local(u, j):
        return local(fin.at[j % 2], grad_out.at[own_block(j)], fin_sem.at[j % 2])

    def fin_remote(u, j):
        return remote(
            fin.at[j % 2], grad_out.at[own_block(j)], fin_send.at[u], fin_recv.at[u], place.twin()
        )

    def fin_wait(u, j, layer):
        @pl.when(core == layer)
        def _():
            fin_local(u, j).wait()

        @pl.when(core != layer)
        def _():
            fin_remote(u, j).wait_send()

    def arrive(k, u, j):
        parity = j % 2
        if k == 0:
            sib_send(u, parity).wait_recv()
        else:
            for step in steps(parity, k - 1):
                hop(u, j, parity, k - 1, step).wait_recv()
        for load in tmp_load(k, u, parity):
            load.start()

    def add_over(slot, parity, k, where, sources):
        order = order_of(parity)
        free = [axis for axis in range(3) if isinstance(where[axis], slice)]
        sizes = [dims[axis] for axis in free]
        total = 1
        for size in sizes:
            total *= size

        def body(i):
            rest = i
            found = {}
            for axis, size in reversed(list(zip(free, sizes))):
                found[axis] = lax.rem(rest, size)
                rest = rest // size
            index = tuple(found[a] if a in found else where[a] for a in range(3))
            spot = (slot,) + index
            value = stage[spot].astype(FULL)
            for source in sources:
                value += source(index).astype(FULL)
            stage[spot] = value.astype(HALF)

        if total == 1:
            body(0)
        else:
            loop(total, body)

    def process(k, u, j, layer):
        parity = j % 2
        order = order_of(parity)
        for load in tmp_load(k, u, parity):
            load.wait()
        if k == 0:
            sources = [lambda index: tmp_s[index]]
        elif k == 1:
            sources = [
                lambda index, step=step: tmp_0[step - 1, index[0], index[order[1]]]
                for step in steps(parity, 0)
            ]
        elif k == 2:
            sources = [
                lambda index, step=step: tmp_1[step - 1, index[0]] for step in steps(parity, 1)
            ]
        if k < 3:
            for step in steps(parity, k):
                add_over(j, parity, k, region(order, k, step), sources)
                hop(u, j, parity, k, step).start()
            add_over(j, parity, k, region(order, k, 0), sources)
        else:

            def free(v, w, its):
                fin_wait(v, w, its)

            if isinstance(u, int):
                if u >= 2:
                    free(u - 2, (j - 2) % 8, 1 - (u - 2) // 8)
            else:

                @pl.when(u >= 2)
                def _():
                    free(u - 2, (j - 2) % 8, 1 - (u - 2) // 8)

            value = stage[(j,) + at].astype(FULL)
            for step in steps(parity, 2):
                value += tmp_2[step - 1].astype(FULL)
            fin[j % 2] = value

            @pl.when(core == layer)
            def _():
                fin_local(u, j).start()

            @pl.when(core != layer)
            def _():
                fin_remote(u, j).start()

            for kk in range(3):
                for step in steps(parity, kk):
                    hop(u, j, parity, kk, step).wait_send()

    def sum_step(it, j):
        todo = []
        for k in range(4):
            back = j - LAGS[k]
            todo.append((k, it * 8 + back, back % 8, back >= 0))

        def guarded(fn):
            for k, u, jj, sure in todo:
                layer = (1 - it) if sure else (2 - it)
                if sure:
                    fn(k, u, jj, layer)
                else:

                    @pl.when(it > 0)
                    def _():
                        fn(k, u, jj, layer)

        guarded(lambda k, u, jj, layer: arrive(k, u, jj))
        guarded(process)

    def flush_step(t):
        todo = [(k, t - LAGS[k]) for k in range(4) if 0 <= t - LAGS[k] < 16]
        for k, u in todo:
            arrive(k, u, u % 8)
        for k, u in todo:
            process(k, u, u % 8, 1 - u // 8)

    def rows_of(slot, n):
        return ws[slot, n].reshape(chunk, D)

    def side(j, which):
        return jnp.where(core == which, j, SLOTS + j % 2)

    def outer(index, left, right):
        def body(n):
            value = nn_dot(left[tile(n, chunk), :], right[...])
            stage[index, n] = value.astype(HALF).reshape(dims[1], dims[2], rank, D)

        loop(dims[0], body)

    def back(dst, terms, fresh, as_half=False):
        def body(n):
            cols = tile(n, chunk)
            total = None
            for left, slot in terms:
                part = nt_dot(left[...], rows_of(slot, n))
                total = part if total is None else total + part
            if not fresh:
                total += dst[:, cols]
            dst[:, cols] = total.astype(HALF) if as_half else total

        loop(dims[0], body)

    def pair_free(it, j):
        if j >= 2:
            sib_send(it * 8 + j - 2, j % 2).wait_send()
        else:

            @pl.when(it > 0)
            def _():
                sib_send(it * 8 + j - 2, j % 2).wait_send()

    def emit(it, j):
        sib_send(it * 8 + j, j % 2).start()
        sum_step(it, j)

    def norm_back(layer, j, last):
        gain = vec[layer, pl.ds(j, 1), :]
        load_xh(layer, j).wait()

        def body(i, carry):
            gains, total = carry
            rows = tile(i, ROWS)
            d = dx[rows, :]
            hat = xh[rows, :]
            dn = d * gain
            first = jnp.mean(dn, -1, keepdims=True)
            second = jnp.mean(dn * hat, -1, keepdims=True)
            out = g[rows, :] + rstd[layer, j, rows, :][:, :1] * (dn - first - hat * second)
            g[rows, :] = out
            gb[rows, :] = out.astype(HALF)
            gains = gains + jnp.sum((d * hat).reshape(ROWS // 8, 8, D), 0)
            if last:
                dxb[layer, rows, :] = out.astype(HALF)
                total = total + jnp.sum(out.reshape(ROWS // 8, 8, D), 0)
            return gains, total

        zero = jnp.zeros((8, D), FULL)
        gains, total = lax.fori_loop(0, SEQ // ROWS, body, (zero, zero))
        sm[0, layer, pl.ds(j, 1), :] = jnp.sum(gains, 0, keepdims=True)
        if last:
            whole = jnp.sum(total, 0, keepdims=True)
            sm[0, layer, pl.ds(3, 1), :] = jnp.where(kind == 1, 0.0, whole)
            sm[0, layer, pl.ds(4, 1), :] = jnp.where(kind == 1, whole, 0.0)

    def attend_back(layer, which, count, causal):
        def pair(hp):
            cols = tile(hp, 128)
            q2 = qkv[0, :, cols] * jnp.asarray(0.125, HALF)
            k2 = qkv[1, :, cols]
            v2 = qkv[2, :, cols]
            do2 = work[3, :, cols]
            kt = k2.T
            dk = [None, None]
            dv = [None, None]
            dq = []

            def put(acc, value, keys):
                for h in range(keys // TILE):
                    piece = value[h * TILE : (h + 1) * TILE]
                    acc[h] = piece if acc[h] is None else acc[h] + piece

            for a in range(2):
                half = lane_half(a)
                ka, va, qa, da = k2 * half, v2 * half, q2 * half, do2 * half
                parts = []
                for first in range(0, SEQ, TILE):
                    span = slice(first, first + TILE)
                    keys = first + TILE if causal else SEQ
                    s = nt_dot(ka[:keys], q2[span])
                    shift = lse[layer, which, hp, pl.ds(a, 1), pl.ds(first, TILE)]
                    p = jnp.where(allowed(keys, first, count, causal), jnp.exp(s - shift), 0.0)
                    dp = nt_dot(va[:keys], do2[span])
                    mix = jnp.sum(dp * p, 0, keepdims=True)
                    ds = (p * (dp - mix)).astype(HALF)
                    put(dv, nn_dot(p.astype(HALF), da[span]), keys)
                    put(dk, nn_dot(ds, qa[span]), keys)
                    parts.append(nn_dot(kt[a * 64 : a * 64 + 64, :keys], ds))
                dq.append(jnp.concatenate(parts, 1))
            whole = jnp.concatenate(dq, 0) * 0.125
            work[0, :, cols] = whole.T.astype(HALF)
            for h in range(SEQ // TILE):
                rows = pl.ds(h * TILE, TILE)
                work[1, rows, cols] = dk[h].astype(HALF)
                work[2, rows, cols] = dv[h].astype(HALF)

        loop(HEADS // 2, pair)

    def give(layer, src, dst, base):
        @pl.when(core == layer)
        def _():
            local(src.at[layer], dst.at[mine], out_sem.at[base]).start()

        @pl.when(core != layer)
        def _():
            remote(
                src.at[layer], dst.at[mine], out_sem.at[base + 1], out_sem.at[base + 2],
                place.twin(),
            ).start()

    def give_done(src, dst, base):
        local(src.at[core], dst.at[mine], out_sem.at[base]).wait()
        remote(
            src.at[other], dst.at[mine], out_sem.at[base + 1], out_sem.at[base + 2], place.twin()
        ).wait_send()
        remote(
            src.at[core], dst.at[twins], out_sem.at[base + 1], out_sem.at[base + 2], place.twin()
        ).wait_recv()

    for slot, b in ((0, 12), (1, 8), (2, 13), (3, 9)):
        load_w(slot, 1, b).start()

    def layer_body(it):
        l = 1 - it
        count_self = meta[0, core]
        count_cross = meta[2, core]

        @pl.when(core == l)
        def _():
            local(cot.at[mine], dxb.at[l], cot_sem.at[0]).start()

        @pl.when(core != l)
        def _():
            remote(
                cot.at[mine], cot_land, cot_swap.at[0], cot_swap.at[1], place.twin()
            ).wait_recv()
            local(cot_land, dxb.at[l], cot_sem.at[0]).start()

        for slot in range(2):
            load_dg(slot, l, slot).start()
        load_xt(0, l, 5).start()
        for q in range(2):
            load_act(1 + q, l, q).start()
        load_xt(3, l, 2).start()
        for i in range(3):
            load_six(i, l, 3 + i).start()
        load_xh(l, 2).start()
        local(cot.at[mine], dxb.at[l], cot_sem.at[0]).wait()

        def begin(i):
            rows = tile(i, ROWS)
            value = dxb[l, rows, :].astype(FULL)
            value = value + jnp.where(it > 0, dxb[1, rows, :].astype(FULL), 0.0)
            g[rows, :] = value
            gb[rows, :] = value.astype(HALF)

        loop(SEQ // ROWS, begin)

        for q in range(4):
            pair = 2 * (q % 2)
            pair_free(it, q)
            load_w(pair, l, 12 + q).wait()
            load_dg(q % 2, l, q).wait()

            def down(n, q=q, pair=pair):
                cols = tile(n, chunk)
                d = nt_dot(gb[...], rows_of(pair, n))
                work[3, :, cols] = (d * work[q % 2, :, cols].astype(FULL)).astype(HALF)

            loop(dims[0], down)
            load_act(1 + q % 2, l, q).wait()
            outer(side(q, 0), xtb.at[1 + q % 2], gb)
            if q == 0:
                load_xt(0, l, 5).wait()
            outer(side(q, 1), xtb.at[0], work.at[3])
            emit_after = q
            load_w(pair + 1, l, 8 + q).wait()
            back(dx, [(work.at[3], pair + 1)], q == 0)
            if q < 2:
                load_w(pair, l, 14 + q).start()
                load_w(pair + 1, l, 10 + q).start()
                load_dg(q, l, q + 2).start()
                load_act(1 + q, l, q + 2).start()
            elif q == 2:
                load_w(0, l, 7).start()
                load_w(1, l, 6).start()
                load_xt(1, l, 4).start()
            else:
                load_w(2, l, 4).start()
                load_w(3, l, 5).start()
                load_xt(2, l, 3).start()
                load_xt(0, l, 1).start()
            emit(it, emit_after)
        norm_back(l, 2, False)
        load_xh(l, 1).start()

        load_w(0, l, 7).wait()
        back(work.at[3], [(gb, 0)], True, True)
        load_w(0, l, 3).start()
        for i in range(3):
            load_six(i, l, 3 + i).wait()
        attend_back(l, 1, count_cross, False)
        for i in range(3):
            load_six(i, l, i).start()
        pair_free(it, 4)
        load_xt(3, l, 2).wait()
        outer(side(4, 0), xtb.at[3], work.at[1])
        outer(side(4, 1), xtb.at[3], work.at[2])
        load_xt(3, l, 0).start()
        emit(it, 4)
        load_w(2, l, 4).wait()
        load_w(3, l, 5).wait()
        back(deb.at[l], [(work.at[1], 2), (work.at[2], 3)], True, True)
        load_w(2, l, 0).start()
        load_w(3, l, 1).start()
        give(l, deb, de_out, 3)
        pair_free(it, 5)
        load_xt(1, l, 4).wait()
        outer(side(5, 0), xtb.at[1], gb)
        load_xt(2, l, 3).wait()
        outer(side(5, 1), xtb.at[2], work.at[0])
        emit(it, 5)
        load_w(1, l, 6).wait()
        back(dx, [(work.at[0], 1)], True)
        load_w(1, l, 2).start()
        norm_back(l, 1, False)
        load_xh(l, 0).start()

        load_w(0, l, 3).wait()
        back(work.at[3], [(gb, 0)], True, True)

        @pl.when(it == 0)
        def _():
            load_w(0, 0, 12).start()

        for i in range(3):
            load_six(i, l, i).wait()
        attend_back(l, 0, count_self, True)
        pair_free(it, 6)
        load_xt(0, l, 1).wait()
        outer(side(6, 0), xtb.at[0], gb)
        load_xt(3, l, 0).wait()
        outer(side(6, 1), xtb.at[3], work.at[0])
        emit(it, 6)
        pair_free(it, 7)
        outer(side(7, 0), xtb.at[3], work.at[1])
        outer(side(7, 1), xtb.at[3], work.at[2])
        emit(it, 7)
        load_w(1, l, 2).wait()
        load_w(2, l, 0).wait()
        load_w(3, l, 1).wait()
        back(dx, [(work.at[0], 2), (work.at[1], 3), (work.at[2], 1)], True)

        @pl.when(it == 0)
        def _():
            load_w(1, 0, 8).start()
            load_w(2, 0, 13).start()
            load_w(3, 0, 9).start()

        norm_back(l, 0, True)
        give(l, dxb, dx_out, 0)

    loop(2, layer_body)

    axes = (2, 1, 0)

    def small_hop(k, step, base):
        return remote(
            sm.at[k + 1],
            sm_land.at[base],
            small_send.at[base],
            small_recv.at[base],
            place.peer(axes[k], step),
        )

    def small_twin():
        return remote(sm.at[0], sm_land.at[0], small_send.at[0], small_recv.at[0], place.twin())

    def bases(k):
        first = 1
        for axis in axes[:k]:
            first += dims[axis] - 1
        return [(step, first + step - 1) for step in range(1, dims[axes[k]])]

    def small_event(k):
        if k == 0:
            small_twin().start()
            return
        if k == 1:
            small_twin().wait_recv()
            sm[1] = sm[0] + sm_land[0]
        else:
            value = sm[k - 1]
            for step, base in bases(k - 2):
                small_hop(k - 2, step, base).wait_recv()
                value += sm_land[base]
            if k == 4:
                small_out[...] = value
                return
            sm[k] = value
        for step, base in bases(k - 1):
            small_hop(k - 1, step, base).start()

    for e in range(max(LAGS)):
        if e < 5:
            small_event(e)
        flush_step(16 + e)
    for e in range(max(LAGS), 5):
        small_event(e)

    small_twin().wait_send()
    for k in range(3):
        for step, base in bases(k):
            small_hop(k, step, base).wait_send()
    cot_send.wait_send()
    for u in (14, 15):
        sib_send(u, u % 2).wait_send()
        fin_wait(u, u % 8, 1 - u // 8)
    for j in range(8):
        unit = (1 - core) * 8 + j
        remote(
            fin.at[j % 2],
            grad_out.at[twin_block(j)],
            fin_send.at[unit],
            fin_recv.at[unit],
            place.twin(),
        ).wait_recv()
    give_done(dxb, dx_out, 0)
    give_done(deb, de_out, 3)


def run_backward(dims, meta, cot, w_all, saved):
    rank = D // (dims[0] * dims[1] * dims[2])
    anyw = pl.BlockSpec(memory_space=pl.ANY)
    vmem = pl.BlockSpec(memory_space=pltpu.VMEM)
    hops = max(dims) - 1
    wide = max(dims[1:])
    smalls = 1 + sum(size - 1 for size in dims)
    dma = pltpu.SemaphoreType.DMA
    shape = jax.ShapeDtypeStruct
    return pl.pallas_call(
        functools.partial(backward_kernel, dims),
        out_shape=(
            shape((2 * SEQ, D), HALF),
            shape((2 * SEQ, D), HALF),
            shape((16, rank, D), FULL),
            shape((2, 8, D), FULL),
            shape((SEQ, D), HALF),
            shape((16,) + dims + (rank, D), HALF),
            shape((16, wide - 1, dims[0], wide, rank, D), HALF),
            shape((16, wide - 1, dims[0], rank, D), HALF),
            shape((16, dims[0] - 1, rank, D), HALF),
        ),
        in_specs=[pl.BlockSpec(memory_space=pltpu.SMEM)] + [anyw] * 7 + [vmem] * 3,
        out_specs=(anyw, anyw, anyw, vmem) + (anyw,) * 5,
        scratch_shapes=[
            pltpu.VMEM((SLOTS + 2,) + dims + (rank, D), HALF),
            pltpu.VMEM((4,) + dims + (rank, D), HALF),
            pltpu.VMEM((SEQ, D), FULL),
            pltpu.VMEM((SEQ, D), FULL),
            pltpu.VMEM((SEQ, D), HALF),
            pltpu.VMEM((3, SEQ, D), HALF),
            pltpu.VMEM((4, SEQ, D), HALF),
            pltpu.VMEM((4, D, SEQ), HALF),
            pltpu.VMEM((SEQ, D), FULL),
            pltpu.VMEM(dims + (rank, D), HALF),
            pltpu.VMEM((wide - 1, dims[0], wide, rank, D), HALF),
            pltpu.VMEM((wide - 1, dims[0], rank, D), HALF),
            pltpu.VMEM((dims[0] - 1, rank, D), HALF),
            pltpu.VMEM((2, SEQ, D), HALF),
            pltpu.VMEM((2, SEQ, D), HALF),
            pltpu.VMEM((2, rank, D), FULL),
            pltpu.VMEM((4, 2, 8, D), FULL),
            pltpu.VMEM((smalls, 2, 8, D), FULL),
            dma((4,)),
            dma((3,)),
            dma((4,)),
            dma((2,)),
            dma((1,)),
            dma((1,)),
            dma((2,)),
            dma((16,)),
            dma((16,)),
            dma((16, 3, hops)),
            dma((16, 3, hops)),
            dma((4, hops)),
            dma((2,)),
            dma((16,)),
            dma((16,)),
            dma((6,)),
            dma((smalls,)),
            dma((smalls,)),
        ],
        compiler_params=pltpu.CompilerParams(
            collective_id=1, has_side_effects=True, vmem_limit_bytes=63 * 2**20
        ),
        cost_estimate=pl.CostEstimate(
            flops=80 * 10**9, bytes_accessed=4 * 10**8, transcendentals=10**7
        ),
    )(meta, cot, w_all, *saved)


def per_device(
    inputs,
    qkv_weight,
    out_weight,
    cross_query,
    cross_kv,
    cross_out,
    ffn_in,
    ffn_out,
    norm_gains,
    type_embed,
    encoder,
    lengths,
    seq_types,
    enc_mask,
    cotangent,
):
    chips = lax.axis_size("dp")
    dims = grid_of(chips)
    rank = D // chips
    pack = packed(
        qkv_weight, out_weight, cross_query, cross_kv, cross_out, ffn_in, ffn_out, chips
    )
    small = small_block(norm_gains, type_embed)
    meta = jnp.stack([lengths, seq_types, jnp.sum(enc_mask, 1)])
    w_all, outs, *saved = run_forward(dims, meta, pack, small, inputs, encoder[0])
    grads = run_backward(dims, meta, cotangent[0], w_all, saved)
    d_in, d_mem, blocks, sums = grads[:4]

    def columns(first, last):
        return jnp.moveaxis(blocks[first:last], 0, 1).reshape(1, rank, -1)

    inner = blocks[8:12].reshape(4, rank, chips, rank).transpose(1, 2, 0, 3)
    own = lax.dynamic_index_in_dim(sums, lax.axis_index("section"), 0, keepdims=False)
    own = lax.dynamic_slice_in_dim(own, lax.axis_index("dp") * rank, rank, 1)
    return (
        outs[None],
        d_in[None],
        d_mem[None],
        columns(0, 3),
        blocks[3:4],
        blocks[6:7],
        columns(4, 6),
        blocks[7:8],
        inner.reshape(1, rank, 4 * D),
        blocks[12:16].reshape(1, 4 * rank, D),
        own[None, :3],
        own[None, 3:5],
    )


def solution(mesh):
    rows = P("section", "dp", None)
    cols = P("section", None, "dp")
    in_specs = (
        (P("dp", None),)
        + (rows,) * 7
        + (cols, cols, rows, P("dp"), P("dp"), P("dp", None), rows)
    )
    out_specs = (rows,) * 10 + (cols, cols)
    return jax.shard_map(
        per_device, mesh=mesh, in_specs=in_specs, out_specs=out_specs, check_vma=False
    )
```

```python
import functools

import jax
import jax.numpy as jnp
from jax import lax
from jax.experimental import pallas as pl
from jax.experimental.pallas import tpu as pltpu
from jax.sharding import PartitionSpec as P

D = 1024
HEADS = 16
SEQ = 512
EPS = 1e-05
NEG = -1e30
MESH = pl.DeviceIdType.MESH
HALF = jnp.bfloat16
FULL = jnp.float32
TILE = 256
ROWS = 128


def grid_of(n):
    deep = 4 if n % 4 == 0 else 1
    rest = n // deep
    wide = max(k for k in range(1, rest + 1) if rest % k == 0 and k * k <= rest)
    return (deep, wide, rest // wide)


class Place:
    def __init__(self, dims):
        self.dims = dims
        self.chip = lax.axis_index("dp")
        self.core = lax.axis_index("section")
        self.other = 1 - self.core
        deep, wide, long = dims
        self.at = (
            self.chip // (wide * long),
            lax.rem(self.chip // long, wide),
            lax.rem(self.chip, long),
        )

    def shifted(self, axis, step):
        where = list(self.at)
        where[axis] = lax.rem(self.at[axis] + step + self.dims[axis], self.dims[axis])
        return where

    def peer(self, axis, step):
        where = self.shifted(axis, step)
        return (self.core, (where[0] * self.dims[1] + where[1]) * self.dims[2] + where[2])

    def twin(self):
        return (self.other, self.chip)

    def greet(self):
        barrier = pltpu.get_barrier_semaphore()
        peers = [self.peer(a, s) for a in range(3) for s in range(1, self.dims[a])]
        peers.append(self.twin())
        for peer in peers:
            pl.semaphore_signal(barrier, inc=1, device_id=peer, device_id_type=MESH)
        pl.semaphore_wait(barrier, len(peers))


def remote(src, dst, send, recv, peer):
    return pltpu.make_async_remote_copy(
        src_ref=src, dst_ref=dst, send_sem=send, recv_sem=recv, device_id=peer, device_id_type=MESH
    )


def local(src, dst, sem):
    return pltpu.make_async_copy(src, dst, sem)


def nt_dot(left, right):
    return lax.dot_general(
        left, right, (((1,), (1,)), ((), ())), preferred_element_type=FULL
    )


def nn_dot(left, right):
    return jnp.dot(left, right, preferred_element_type=FULL)


def tile(i, size=TILE):
    return pl.ds(pl.multiple_of(i * size, size), size)


def loop(count, body):
    def step(i, carry):
        body(i)
        return carry

    lax.fori_loop(0, count, step, 0)


def lane_half(a):
    lane = lax.broadcasted_iota(jnp.int32, (1, 128), 1)
    return jnp.where((lane // 64) == a, 1.0, 0.0).astype(HALF)


def allowed(keys, first, count, causal):
    key = lax.broadcasted_iota(jnp.int32, (keys, TILE), 0)
    ok = key < count
    if causal:
        ok = ok & (key <= first + lax.broadcasted_iota(jnp.int32, (keys, TILE), 1))
    return ok


ORDER_A = (0, 2, 1)
ORDER_B = (0, 1, 2)
ORDER_C = (2, 0, 1)
ORDER_D = (1, 0, 2)
DEEP_SLOTS = 5
MARGIN = 1.0


def deep_sends(k):
    if k == 0:
        return [
            (0, lambda z: z < 3, 1),
            (1, lambda z: z > 0, -1),
            (2, lambda z: z < 2, 2),
            (3, lambda z: z > 1, -2),
        ]
    return [(4, lambda z: z == 2, 1), (4, lambda z: z == 1, -1)]


def stages_of(order):
    found = []
    for axis in order:
        found += [(axis, 0), (axis, 1)] if axis == 0 else [(axis, 0)]
    return found


class Plan:
    UNIT = 2.85
    LATENCY = 2.0

    def __init__(self):
        self.free = {}
        self.time = 0.0
        self.queue = []
        self.count = 0

    def push(self, ready, event):
        self.queue.append((ready, self.count, event))
        self.count += 1

    def occupy(self, loads):
        end = self.time
        for link, load in loads:
            begin = max(self.time, self.free.get(link, 0.0))
            self.free[link] = begin + load
            end = max(end, begin + load)
        return end + self.LATENCY

    def pop(self, before, allowed=lambda event: True):
        ready = [item for item in self.queue if item[0] <= before and allowed(item[2])]
        if not ready:
            return None
        item = min(ready)
        self.queue.remove(item)
        self.time = max(self.time, item[0])
        return item[2]


def stage_loads(order, k, gather):
    stages = stages_of(order)
    axis, part = stages[k]
    size = (4, 2, 2)
    if gather:
        held = 1
        for other in set(a for a, _ in stages[:k]):
            if other != axis:
                held *= size[other]
    else:
        held = 16
        for other in set(a for a, _ in stages[: k + 1]):
            held //= size[other]
    if axis != 0:
        return [(axis, held * Plan.UNIT)]
    far, near = ("middle", "end") if gather else ("end", "middle")
    if part == 0:
        return [(far, 3 * held * Plan.UNIT), (near, 2 * held * Plan.UNIT)]
    return [(near, held * Plan.UNIT)]


FORWARD_CHUNKS = (
    [(4, None), (2, 0), (1.5, 0), (1.5, 0)] + [(2, 0)] * 4 + [(2, 0), (4, None)]
    + [(2.5, 1), (1.5, 1), (1.5, 1)] + [(2, 1)] * 4 + [(2, 1), (3, None)]
    + [(4, 2)] + [(3.5, 2)] * 3 + [(7, 3)]
)
GATHER_ORDERS = (
    ORDER_A, ORDER_B, ORDER_C, ORDER_D, ORDER_A, ORDER_B, ORDER_C, ORDER_D,
    ORDER_A, ORDER_B, ORDER_C, ORDER_D, ORDER_A, ORDER_B, ORDER_C, ORDER_D,
)
GATHER_WINDOW = 3
GATHER_STAGE = 2


def plan_forward():
    plan = Plan()
    after = {}
    for u in range(GATHER_WINDOW):
        plan.push(0.0, (u, 0))
    following = GATHER_WINDOW
    plan.push(0.0, (-1, 0))
    done = set()

    def take(event, out):
        nonlocal following
        u, k = event
        plan.time += 0.4
        done.add(event)
        out.append(event)
        if u < 0:
            if k < 4:
                plan.push(plan.time + 3.0, (u, k + 1))
            return
        if k < 4:
            loads = stage_loads(GATHER_ORDERS[u], k, True)
            plan.push(plan.occupy(loads), (u, k + 1))
        elif k == 4:
            plan.push(plan.occupy([("twin", 4.0)]), (u, 5))
        if k == GATHER_STAGE and following < 16:
            plan.push(plan.time, (following, 0))
            following += 1

    for layer in range(2):
        for i, (length, group) in enumerate(FORWARD_CHUNKS):
            out = []
            while True:
                event = plan.pop(plan.time - MARGIN)
                if event is None:
                    break
                take(event, out)
            need = [(-1, 4)]
            if group is not None:
                first = 2 * (4 * layer + group)
                need += [(first, 5), (first + 1, 5)]
            while not done.issuperset(need):
                take(plan.pop(1e9), out)
            plan.time += length
            after[layer, i] = out
    assert not plan.queue and following == 16
    return after, plan.time


def forward_kernel(
    dims,
    meta,
    pack,
    small,
    hidden,
    frames,
    w_all,
    y_out,
    six_out,
    xt_out,
    actt_out,
    dg_out,
    xh_out,
    rstd_out,
    lse_out,
    vec_out,
    ws,
    res,
    xb,
    mem,
    six,
    xt,
    actn,
    actt,
    dg,
    xh,
    hin,
    yb,
    vecs,
    seed_sem,
    swap_send,
    swap_recv,
    hop_send,
    hop_recv,
    twin_send,
    twin_recv,
    vec_send,
    vec_recv,
    vec_swap,
    in_sem,
    frame_sem,
    y_sem,
    w_sem,
    save_sem,
):
    place = Place(dims)
    core, other, at = place.core, place.other, place.at
    place.greet()

    def seed(g):
        return local(
            pack.at[g, pl.ds(2 * core, 2)],
            w_all.at[pl.ds((core * 4 + g) * 4 + 2 * core, 2), at[0], at[1], at[2]],
            seed_sem.at[g],
        )

    def swap(g):
        return remote(
            pack.at[g, pl.ds(2 * other, 2)],
            w_all.at[pl.ds((core * 4 + g) * 4 + 2 * other, 2), at[0], at[1], at[2]],
            swap_send.at[g],
            swap_recv.at[g],
            place.twin(),
        )

    def swapped(layer, g):
        spot = w_all.at[pl.ds((layer * 4 + g) * 4 + 2 * core, 2), at[0], at[1], at[2]]
        return remote(spot, spot, swap_send.at[g], swap_recv.at[g], place.twin())

    own_vec = vecs.at[core, at[0], at[1], at[2]]
    vec_in = local(small, own_vec, in_sem.at[0])
    vec_in.start()
    mine = pl.ds(core * SEQ, SEQ)
    twins = pl.ds(other * SEQ, SEQ)
    hid_in = local(hidden.at[mine], hin, in_sem.at[1])
    hid_in.start()
    mem_in = local(frames.at[mine], mem.at[core], in_sem.at[2])
    mem_in.start()
    for g in range(4):
        seed(g).start()
        swap(g).start()
    mem_swap = remote(
        frames.at[twins], mem.at[core], frame_sem.at[0], frame_sem.at[1], place.twin()
    )
    mem_swap.start()

    def block_of(u):
        return (u // 2) * 4 + 2 * core + u % 2

    def part(order, k, place_of):
        axis = stages_of(order)[k][0]
        index = []
        for other_axis in range(3):
            if other_axis == axis:
                index.append(place_of)
            elif other_axis in [a for a, _ in stages_of(order)[:k]]:
                index.append(slice(None))
            else:
                index.append(at[other_axis])
        return tuple(index)

    def stage_copies(order, k, base, prefix, send, recv, sending):
        axis, piece = stages_of(order)[k]
        found = []
        if axis != 0:
            for step in range(1, dims[axis]):
                where = place.shifted(axis, 0 if sending else -step)[axis]
                ref = base.at[prefix + part(order, k, where)]
                sems = (send.at[axis, step - 1], recv.at[axis, step - 1])
                found.append((None, remote(ref, ref, *sems, place.peer(axis, step))))
            return found
        if dims[0] == 1:
            return found
        for slot, test, step in deep_sends(piece):
            sems = (send.at[0, slot], recv.at[0, slot])
            if sending:
                from_z = at[0] if piece == 0 else (0 if step > 0 else dims[0] - 1)
                okay = test(at[0])
            else:
                from_z = at[0] - step if piece == 0 else (0 if step > 0 else dims[0] - 1)
                okay = test(at[0] - step) & (at[0] - step >= 0) & (at[0] - step < dims[0])
                from_z = jnp.clip(from_z, 0, dims[0] - 1)
            ref = base.at[prefix + part(order, k, from_z)]
            found.append((okay, remote(ref, ref, *sems, place.peer(0, step))))
        return found

    def each(copies, act):
        for okay, copy in copies:
            if okay is None:
                act(copy)
            else:
                pl.when(okay)(functools.partial(act, copy))

    def hops_of(u, k, sending):
        return stage_copies(
            GATHER_ORDERS[u], k, w_all, (block_of(u),), hop_send.at[u], hop_recv.at[u], sending
        )

    def vec_hops(k, sending):
        return stage_copies(ORDER_B, k, vecs, (core,), vec_send, vec_recv, sending)

    def twin_copy(u, block):
        return remote(
            w_all.at[block], w_all.at[block], twin_send.at[u], twin_recv.at[u], place.twin()
        )

    def vec_twin(layer):
        return remote(
            vecs.at[layer], vecs.at[layer], vec_swap.at[0], vec_swap.at[1], place.twin()
        )

    def event(u, k):
        if u < 0:
            if k == 0:
                vec_in.wait()
            else:
                each(vec_hops(k - 1, False), lambda copy: copy.wait_recv())
            if k < 4:
                each(vec_hops(k, True), lambda copy: copy.start())
            else:
                vec_twin(core).start()
                vec_twin(other).wait_recv()
            return
        layer, g = u // 8, (u // 2) % 4
        if k == 0 and u % 2 == 0:

            @pl.when(core == layer)
            def _():
                seed(g).wait()

            @pl.when(core != layer)
            def _():
                swapped(layer, g).wait_recv()

        if 0 < k <= 4:
            each(hops_of(u, k - 1, False), lambda copy: copy.wait_recv())
        if k < 4:
            each(hops_of(u, k, True), lambda copy: copy.start())
        elif k == 4:
            twin_copy(u, block_of(u)).start()
        else:
            twin_copy(u, (u // 2) * 4 + 2 * other + u % 2).wait_recv()

    events, _ = plan_forward()

    def save_to(layer, kind, i):
        src, dst, first = {
            "six": (six, six_out, 0),
            "xt": (xt, xt_out, 6),
            "actt": (actt, actt_out, 12),
            "dg": (dg, dg_out, 16),
            "xh": (xh, xh_out, 20),
        }[kind]
        return local(src.at[i], dst.at[layer, i], save_sem.at[first + i])

    saves = (
        [("six", i) for i in range(6)]
        + [("xt", i) for i in range(6)]
        + [("actt", i) for i in range(4)]
        + [("dg", i) for i in range(4)]
        + [("xh", i) for i in range(3)]
    )

    def weight(s, cols=slice(None)):
        block = ws[s, :, :, :, :, cols]
        return block.reshape(D, block.shape[-1])

    def early():
        hid_in.wait()
        mem_in.wait()
        remote(
            frames.at[mine], mem.at[other], frame_sem.at[0], frame_sem.at[1], place.twin()
        ).wait_recv()

    count_self = meta[0, core]
    kind = meta[1, core]
    count_cross = meta[2, core]

    def layer_body(l):
        def guard(what, i):
            @pl.when(l > 0)
            def _():
                save_to(l - 1, what, i).wait()

        def save(what, i):
            save_to(l, what, i).start()

        passed = []

        def point():
            i = len(passed)
            passed.append(i)
            for layer in range(2):
                if events[layer, i]:

                    @pl.when(l == layer)
                    def _(layer=layer):
                        for u, k in events[layer, i]:
                            event(u, k)

        def fetch(g):
            for q in range(4):
                local(w_all.at[(l * 4 + g) * 4 + q], ws.at[q], w_sem.at[q]).start()

        def ready(g, q):
            local(w_all.at[(l * 4 + g) * 4 + q], ws.at[q], w_sem.at[q]).wait()

        def flip(src, i):
            guard("xt", i)

            def step(n):
                xt[i, tile(n), :] = src[:, tile(n)].T

            loop(D // TILE, step)
            save("xt", i)

        def norm(j):
            gain = vec_out[l, pl.ds(j, 1), :]
            guard("xh", j)

            def step(i):
                rows = tile(i, ROWS)
                v = res[rows, :]
                cent = v - jnp.mean(v, -1, keepdims=True)
                rstd = lax.rsqrt(jnp.mean(cent * cent, -1, keepdims=True) + EPS)
                hat = cent * rstd
                xh[j, rows, :] = hat
                rstd_out[l, j, rows, :] = jnp.broadcast_to(rstd, (ROWS, 128))
                xb[rows, :] = (hat * gain).astype(HALF)

            loop(SEQ // ROWS, step)
            save("xh", j)

        def project(src, s, i):
            guard("six", i)

            six[i] = nn_dot(src[...], weight(s)).astype(HALF)
            save("six", i)

        def attend(qi, ki, vi, which, out, count, causal):
            guard("xt", out)

            def pair(hp):
                cols = tile(hp, 128)
                q2 = six[qi, :, cols] * jnp.asarray(0.125, HALF)
                k2 = six[ki, :, cols]
                vt = six[vi, :, cols].T
                ka = [k2 * lane_half(a) for a in range(2)]
                for f in range(0, SEQ, TILE):
                    keys = f + TILE if causal else SEQ
                    scores = [nt_dot(ka[a][:keys], q2[f : f + TILE]) for a in range(2)]
                    probs = []
                    for a in range(2):
                        s = jnp.where(allowed(keys, f, count, causal), scores[a], NEG)
                        top = jnp.max(s, 0, keepdims=True)
                        expo = jnp.exp(s - top)
                        total = jnp.sum(expo, 0, keepdims=True)
                        probs.append((expo * (1.0 / total)).astype(HALF))
                        lse_out[l, which, hp, pl.ds(a, 1), pl.ds(f, TILE)] = top + jnp.log(total)
                    for a in range(2):
                        o = nn_dot(vt[a * 64 : a * 64 + 64, :keys], probs[a])
                        xt[out, pl.ds(hp * 128 + a * 64, 64), pl.ds(f, TILE)] = o.astype(HALF)
                xb[:, cols] = xt[out, tile(hp, 128), :].T

            for part_of in range(4):
                if part_of:
                    point()
                loop(HEADS // 8, lambda hp, part_of=part_of: pair(part_of * (HEADS // 8) + hp))
            save("xt", out)

        def add_product(src, s):
            res[...] += nn_dot(src[...], weight(s))

        point()

        @pl.when(l == 0)
        def _():
            early()
            rank = D // (dims[0] * dims[1] * dims[2])
            vec_out[...] = jnp.zeros(vec_out.shape, FULL)

            def step(j):
                row = lax.broadcasted_iota(jnp.int32, (128, D), 0)
                col = lax.broadcasted_iota(jnp.int32, (128, D), 1)
                spread = jnp.where((col == j * rank + row) & (row < rank), 1.0, 0.0).astype(HALF)
                z = j // (dims[1] * dims[2])
                y = lax.rem(j // dims[2], dims[1])
                x = lax.rem(j, dims[2])
                for m in range(2):
                    vec_out[m] += nn_dot(vecs[m, z, y, x], spread)

            loop(dims[0] * dims[1] * dims[2], step)

        shift = jnp.where(kind == 1, vec_out[l, pl.ds(4, 1), :], vec_out[l, pl.ds(3, 1), :])

        def begin(i):
            rows = tile(i, ROWS)
            came = jnp.where(l == 0, hin[rows, :].astype(FULL), yb[0, rows, :].astype(FULL))
            res[rows, :] = came + shift

        loop(SEQ // ROWS, begin)
        norm(0)
        flip(xb, 0)
        point()
        fetch(0)
        for q in range(3):
            if q:
                point()
            ready(0, q)
            project(xb, q, q)
        point()
        attend(0, 1, 2, 0, 1, count_self, True)
        point()
        ready(0, 3)
        add_product(xb, 3)
        point()
        norm(1)
        flip(xb, 3)
        flip(mem.at[l], 2)
        point()
        fetch(1)
        ready(1, 2)
        project(xb, 2, 3)
        point()
        ready(1, 0)
        project(mem.at[l], 0, 4)
        point()
        ready(1, 1)
        project(mem.at[l], 1, 5)
        point()
        attend(3, 4, 5, 1, 4, count_cross, False)
        point()
        ready(1, 3)
        add_product(xb, 3)
        point()
        norm(2)
        flip(xb, 5)
        for q in range(4):
            point()
            if q == 0:
                fetch(2)
            ready(2, q)
            guard("dg", q)
            guard("actt", q)

            for first in range(0, D, 512):
                cols = slice(first, first + 512)
                u = nn_dot(xb[...], weight(q, cols))
                cdf = 0.5 * (1.0 + lax.erf(u * (0.5**0.5)))
                act = (u * cdf).astype(HALF)
                actn[q, :, cols] = act
                actt[q, cols, :] = act.T
                bell = jnp.exp(-0.5 * u * u) * 0.3989422804014327
                dg[q, :, cols] = (cdf + u * bell).astype(HALF)
            save("dg", q)
            save("actt", q)
        point()
        fetch(3)
        for q in range(4):
            ready(3, q)
        assert len(passed) == len(FORWARD_CHUNKS)

        for first in range(0, D, 512):
            cols = slice(first, first + 512)
            total = res[:, cols]
            for q in range(4):
                total += nn_dot(actn[q], weight(q, cols))
            yb[l, :, cols] = total.astype(HALF)

        @pl.when(core == l)
        def _():
            local(yb.at[l], y_out.at[mine], y_sem.at[0]).start()

        @pl.when(core != l)
        def _():
            remote(yb.at[l], y_out.at[mine], y_sem.at[1], y_sem.at[2], place.twin()).start()

    loop(2, layer_body)

    for what, i in saves:
        save_to(1, what, i).wait()
    local(yb.at[core], y_out.at[mine], y_sem.at[0]).wait()
    remote(yb.at[other], y_out.at[mine], y_sem.at[1], y_sem.at[2], place.twin()).wait_send()
    remote(yb.at[core], y_out.at[twins], y_sem.at[1], y_sem.at[2], place.twin()).wait_recv()
    mem_swap.wait_send()
    for g in range(4):
        swap(g).wait_send()
    for k in range(4):
        each(vec_hops(k, True), lambda copy: copy.wait_send())
    vec_twin(core).wait_send()
    for u in range(16):
        for k in range(4):
            each(hops_of(u, k, True), lambda copy: copy.wait_send())
        twin_copy(u, block_of(u)).wait_send()


def run_forward(dims, meta, pack, small, hidden, frames):
    rank = D // (dims[0] * dims[1] * dims[2])
    anyw = pl.BlockSpec(memory_space=pl.ANY)
    vmem = pl.BlockSpec(memory_space=pltpu.VMEM)
    dma = pltpu.SemaphoreType.DMA
    shape = jax.ShapeDtypeStruct
    return pl.pallas_call(
        functools.partial(forward_kernel, dims),
        out_shape=(
            shape((32,) + dims + (rank, D), HALF),
            shape((2 * SEQ, D), HALF),
            shape((2, 6, SEQ, D), HALF),
            shape((2, 6, D, SEQ), HALF),
            shape((2, 4, D, SEQ), HALF),
            shape((2, 4, SEQ, D), HALF),
            shape((2, 3, SEQ, D), FULL),
            shape((2, 3, SEQ, 128), FULL),
            shape((2, 2, HEADS // 2, 2, SEQ), FULL),
            shape((2, 16, D), FULL),
        ),
        in_specs=[pl.BlockSpec(memory_space=pltpu.SMEM), vmem] + [anyw] * 3,
        out_specs=(anyw,) * 7 + (vmem,) * 3,
        scratch_shapes=[
            pltpu.VMEM((4,) + dims + (rank, D), HALF),
            pltpu.VMEM((SEQ, D), FULL),
            pltpu.VMEM((SEQ, D), HALF),
            pltpu.VMEM((2, SEQ, D), HALF),
            pltpu.VMEM((6, SEQ, D), HALF),
            pltpu.VMEM((6, D, SEQ), HALF),
            pltpu.VMEM((4, SEQ, D), HALF),
            pltpu.VMEM((4, D, SEQ), HALF),
            pltpu.VMEM((4, SEQ, D), HALF),
            pltpu.VMEM((3, SEQ, D), FULL),
            pltpu.VMEM((SEQ, D), HALF),
            pltpu.VMEM((2, SEQ, D), HALF),
            pltpu.VMEM((2,) + dims + (16, 128), HALF),
            dma((4,)),
            dma((4,)),
            dma((4,)),
            dma((16, 3, DEEP_SLOTS)),
            dma((16, 3, DEEP_SLOTS)),
            dma((16,)),
            dma((16,)),
            dma((3, DEEP_SLOTS)),
            dma((3, DEEP_SLOTS)),
            dma((2,)),
            dma((3,)),
            dma((2,)),
            dma((3,)),
            dma((4,)),
            dma((23,)),
        ],
        compiler_params=pltpu.CompilerParams(
            collective_id=0, has_side_effects=True, vmem_limit_bytes=60 * 2**20
        ),
        cost_estimate=pl.CostEstimate(
            flops=40 * 10**9, bytes_accessed=3 * 10**8, transcendentals=10**7
        ),
    )(meta, pack, small, hidden, frames)


def packed(qkv_weight, out_weight, cross_query, cross_kv, cross_out, ffn_in, ffn_out, chips):
    rank = qkv_weight.shape[1]

    def columns(w):
        return jnp.moveaxis(w[0].astype(HALF).reshape(rank, -1, D), 1, 0)

    inner = ffn_in[0].astype(HALF).reshape(rank, chips, 4, rank)
    inner = inner.transpose(2, 0, 1, 3).reshape(4, rank, D)
    outer = ffn_out[0].astype(HALF).reshape(4, rank, D)
    first = jnp.concatenate([columns(qkv_weight), columns(out_weight)], 0)
    second = jnp.concatenate([columns(cross_kv), columns(cross_query), columns(cross_out)], 0)
    return jnp.stack([first, second, inner, outer])


def small_block(norm_gains, type_embed):
    rows = jnp.concatenate([norm_gains[0], type_embed[0]], 0).astype(HALF)
    return jnp.pad(rows, ((0, 16 - rows.shape[0]), (0, 128 - rows.shape[1])))


SUM_A = (1, 2, 0)
SUM_B = (2, 1, 0)
SUM_C = (1, 0, 2)
SUM_D = (2, 0, 1)
SUM_ORDERS = (
    SUM_C, SUM_B, SUM_C, SUM_B, SUM_D, SUM_A, SUM_C, SUM_D,
    SUM_D, SUM_A, SUM_C, SUM_C, SUM_D, SUM_B, SUM_C, SUM_B,
)
SLOTS = 7
PAIRS = ((12, 8), (13, 9), (14, 10), (15, 11), (4, 5), (7, 6), (3, 0), (1, 2))


def deep_sums(k):
    if k == 0:
        return [
            (0, lambda z: z < 3, lambda z: z + 1, 1),
            (1, lambda z: z > 0, lambda z: z - 1, -1),
            (2, lambda z: z == 0, lambda z: 2, 2),
            (3, lambda z: z == 3, lambda z: 1, -2),
            (4, lambda z: z == 0, lambda z: 3, 1),
            (4, lambda z: z == 3, lambda z: 0, -1),
        ]
    return [(2, lambda z: z == 1, lambda z: 3, 2), (3, lambda z: z == 2, lambda z: 0, -2)]


BACKWARD_CHUNKS = (
    [(3, None, None)]
    + [
        c
        for q in range(4)
        for c in ((2, None, None), (1.5, q, None), (1.5, None, q), (1.5, None, None))
    ]
    + [(4, None, None)] + [(3.2, None, None)] * 4
    + [(1.5, 4, None), (1.5, None, 4), (3, None, None)]
    + [(1.5, 5, None), (1.5, None, 5), (5, None, None)] + [(2.6, None, None)] * 4
    + [(1.5, 6, None), (1.5, None, 6), (1.5, 7, None), (1.5, None, 7), (6, None, None)]
)


def landing_kind(order, k):
    if k == 0:
        return "s"
    axis, piece = stages_of(order)[k - 1]
    if axis == 0:
        return "z" if piece else "x"
    return "a"


def plan_backward():
    plan = Plan()
    after = {}
    done = set()
    busy = set()

    def allowed(event):
        what, u, k = event
        return what == "p" or landing_kind(SUM_ORDERS[u], k) not in busy

    def take(event, out):
        what, u, k = event
        done.add(event)
        out.append(event)
        if what == "a":
            busy.add(landing_kind(SUM_ORDERS[u], k))
            plan.time += 0.15
            plan.push(plan.time + (1.5 if k == 0 else 0.8), ("p", u, k))
            return
        busy.discard(landing_kind(SUM_ORDERS[u], k))
        plan.time += 1.5 if k == 0 else 0.5
        if k < 4:
            loads = stage_loads(SUM_ORDERS[u], k, False)
            plan.push(plan.occupy(loads), ("a", u, k + 1))

    for it in range(2):
        for i, (length, begun, sent) in enumerate(BACKWARD_CHUNKS):
            out = []
            while True:
                event = plan.pop(plan.time - MARGIN, allowed)
                if event is None:
                    break
                take(event, out)
            last = -1 if begun is None else it * 8 + begun - SLOTS
            if last >= 0:
                while ("p", last, 4) not in done:
                    take(plan.pop(1e9, allowed), out)
            plan.time += length
            if sent is not None:
                plan.push(plan.occupy([("twin", 4.0)]), ("a", it * 8 + sent, 0))
            after[it, i] = out
    rest = []
    while plan.queue:
        take(plan.pop(1e9, allowed), rest)
    return after, rest, plan.time


def backward_kernel(
    dims,
    meta,
    cot,
    w_all,
    six_in,
    xt_in,
    actt_in,
    dg_in,
    xh_in,
    rstd_in,
    lse,
    vec,
    dx_out,
    de_out,
    grad_out,
    small_out,
    cot_land,
    land_s,
    land_a,
    land_b,
    land_z,
    stage,
    ws,
    g,
    dx,
    gb,
    qkv,
    work,
    xtb,
    xh,
    rstd,
    tmp_s,
    tmp_a,
    tmp_z,
    dxb,
    deb,
    fin,
    sm,
    sm_land,
    w_sem,
    six_sem,
    xt_sem,
    dg_sem,
    xh_sem,
    cot_sem,
    cot_swap,
    s_send,
    s_recv,
    hop_send,
    hop_recv,
    tmp_sem,
    fin_sem,
    fin_send,
    fin_recv,
    out_sem,
    small_send,
    small_recv,
):
    place = Place(dims)
    core, other, at = place.core, place.other, place.at
    rank = D // (dims[0] * dims[1] * dims[2])
    place.greet()
    mine = pl.ds(core * SEQ, SEQ)
    twins = pl.ds(other * SEQ, SEQ)
    cot_send = remote(cot.at[twins], cot_land, cot_swap.at[0], cot_swap.at[1], place.twin())
    cot_send.start()
    kind = meta[1, core]

    def load_w(slot, layer, b):
        return local(w_all.at[layer * 16 + b], ws.at[slot], w_sem.at[slot])

    def load_six(slot, layer, i):
        return local(six_in.at[layer, i], qkv.at[slot], six_sem.at[slot])

    def load_xt(slot, layer, i):
        return local(xt_in.at[layer, i], xtb.at[slot], xt_sem.at[slot])

    def load_act(slot, layer, q):
        return local(actt_in.at[layer, q], xtb.at[slot], xt_sem.at[slot])

    def load_dg(slot, layer, q):
        return local(dg_in.at[layer, q], work.at[slot], dg_sem.at[slot])

    def load_xh(layer, j):
        return local(xh_in.at[layer, j], xh, xh_sem.at[0])

    def load_rstd(layer, j):
        return local(rstd_in.at[layer, j], rstd, xh_sem.at[1])

    def region(order, k, value):
        stages = stages_of(order)
        index = []
        for axis in range(3):
            if axis == stages[k][0]:
                index.append(value)
            elif axis in [a for a, _ in stages[:k]]:
                index.append(at[axis])
            else:
                index.append(slice(None))
        return tuple(index)

    def fit(order, k, pool, slot):
        free = [a for a in range(3) if isinstance(region(order, k, 0)[a], slice)]
        if pool is tmp_a and k > 0:
            return slot + ((slice(None),) if free else (0,)) + (0,)
        if pool is land_a or pool is tmp_a:
            return slot + (slice(None), pl.ds(0, dims[free[1]]))
        if pool is land_b:
            return slot + ((slice(None),) if free else (0,))
        return slot + ((pl.ds(0, dims[free[0]]),) if free else (0,))

    def pools(order, k):
        axis = stages_of(order)[k][0]
        if axis == 0:
            return land_z, tmp_z
        return (land_a if k == 0 else land_b), tmp_a

    def sends(u, k):
        order = SUM_ORDERS[u]
        axis, piece = stages_of(order)[k]
        land = pools(order, k)[0]
        found = []
        if axis != 0:
            options = [
                (step - 1, None, place.shifted(axis, step)[axis], step)
                for step in range(1, dims[axis])
            ]
        elif dims[0] == 1:
            options = []
        else:
            options = [
                (slot, test(at[0]), jnp.clip(block(at[0]), 0, dims[0] - 1), step)
                for slot, test, block, step in deep_sums(piece)
            ]
        for slot, okay, value, step in options:
            copy = remote(
                stage.at[(u % SLOTS,) + region(order, k, value)],
                land.at[fit(order, k, land, (u, slot))],
                hop_send.at[u, axis, slot],
                hop_recv.at[u, axis, slot],
                place.peer(axis, step),
            )
            found.append((okay, copy))
        return found

    def came(u, k):
        axis, piece = stages_of(SUM_ORDERS[u])[k - 1]
        if axis != 0:
            return [(step - 1, None) for step in range(1, dims[axis])]
        if dims[0] == 1:
            return []
        if piece == 0:
            return [(4, (at[0] == 1) | (at[0] == 2))]
        return [(0, at[0] >= 1), (1, at[0] <= 2), (2, at[0] >= 2), (3, at[0] <= 1)]

    def when(okay, act):
        if okay is None:
            act()
        else:
            pl.when(okay)(act)

    def arrivals(u, k):
        order = SUM_ORDERS[u]
        axis = stages_of(order)[k - 1][0]
        land, tmp = pools(order, k - 1)
        for slot, okay in came(u, k):
            spot = land.at[fit(order, k - 1, land, (u, slot))]
            wait = functools.partial(
                remote,
                spot,
                spot,
                hop_send.at[u, axis, slot],
                hop_recv.at[u, axis, slot],
                place.twin(),
            )
            load = functools.partial(
                local,
                spot,
                tmp.at[fit(order, k - 1, tmp, (slot,))],
                tmp_sem.at["sabz".index("z" if axis == 0 else ("a" if k == 1 else "b")), slot],
            )
            yield okay, wait, load

    def s_load(u):
        return local(land_s.at[u], tmp_s, tmp_sem.at[0, 0])

    def sib_send(u, parity):
        return remote(
            stage.at[SLOTS + parity], land_s.at[u], s_send.at[u], s_recv.at[u], place.twin()
        )

    def own_block(j):
        return jnp.where(core == 0, PAIRS[j][0], PAIRS[j][1])

    def twin_block(j):
        return jnp.where(core == 0, PAIRS[j][1], PAIRS[j][0])

    def fin_local(u):
        place_of = finals.index(u) % 2
        return local(fin.at[place_of], grad_out.at[own_block(u % 8)], fin_sem.at[place_of])

    def fin_remote(u):
        return remote(
            fin.at[finals.index(u) % 2],
            grad_out.at[own_block(u % 8)],
            fin_send.at[u],
            fin_recv.at[u],
            place.twin(),
        )

    def fin_wait(u):
        layer = 1 - u // 8
        pl.when(core == layer)(lambda: fin_local(u).wait())
        pl.when(core != layer)(lambda: fin_remote(u).wait_send())

    def add_over(slot, where, sources):
        free = [axis for axis in range(3) if isinstance(where[axis], slice)]
        total = 1
        for axis in free:
            total *= dims[axis]

        def body(i):
            found = {}
            for axis in reversed(free):
                found[axis] = lax.rem(i, dims[axis])
                i = i // dims[axis]
            index = tuple(found.get(a, where[a]) for a in range(3))
            spot = (slot,) + index
            if len(sources) == 1 and sources[0][0] is None:
                stage[spot] = stage[spot] + sources[0][1](index)
                return
            value = stage[spot].astype(FULL)
            for okay, source in sources:
                more = source(index).astype(FULL)
                value += more if okay is None else jnp.where(okay, more, 0.0)
            stage[spot] = value.astype(HALF)

        if total == 1:
            body(0)
        else:
            loop(total, body)

    def sources_of(u, k):
        order = SUM_ORDERS[u]
        tmp = pools(order, k - 1)[1]
        axis = stages_of(order)[k - 1][0]
        free = [a for a in range(3) if isinstance(region(order, k - 1, 0)[a], slice)]

        def source(slot):
            def read(index):
                if tmp is tmp_a and k > 1:
                    return tmp[slot, index[free[0]] if free else 0, 0]
                if tmp is tmp_a:
                    return tmp[slot, index[free[0]], index[free[1]]]
                return tmp[slot, index[free[0]] if free else 0]

            return read

        return [(okay, source(slot)) for slot, okay in came(u, k)]

    def sum_event(what, u, k):
        order = SUM_ORDERS[u]
        slot = u % SLOTS
        if what == "a":
            if k == 0:
                sib_send(u, u % 2).wait_recv()
                s_load(u).start()
                return
            for okay, wait, load in arrivals(u, k):

                def act(wait=wait, load=load):
                    wait().wait_recv()
                    load().start()

                when(okay, act)
            return
        if k == 0:
            axis = order[0]
            s_load(u).wait()
            sources = [(None, lambda index: tmp_s[index])]
            for (okay, copy), step in zip(sends(u, 0), range(1, dims[axis])):
                add_over(slot, region(order, 0, place.shifted(axis, step)[axis]), sources)
                copy.start()
            add_over(slot, region(order, 0, at[axis]), sources)
            return
        for okay, _, load in arrivals(u, k):
            when(okay, lambda load=load: load().wait())
        sources = sources_of(u, k)
        axis, piece = stages_of(order)[k - 1]
        if k < 4:
            if axis == 0 and piece == 0:
                if sources:
                    far = jnp.where(at[0] == 1, dims[0] - 1, 0)
                    pl.when(sources[0][0])(
                        lambda: add_over(slot, region(order, k - 1, far), [(None, sources[0][1])])
                    )
            elif sources:
                add_over(slot, region(order, k - 1, at[axis]), sources)
            for okay, copy in sends(u, k):
                when(okay, lambda copy=copy: copy.start())
            return
        turn = finals.index(u)
        if turn >= 2:
            fin_wait(finals[turn - 2])
        value = stage[(slot,) + at].astype(FULL)
        for okay, source in sources:
            more = source(at).astype(FULL)
            value += more if okay is None else jnp.where(okay, more, 0.0)
        fin[turn % 2] = value
        layer = 1 - u // 8
        pl.when(core == layer)(lambda: fin_local(u).start())
        pl.when(core != layer)(lambda: fin_remote(u).start())
        for kk in range(4):
            for okay, copy in sends(u, kk):
                when(okay, lambda copy=copy: copy.wait_send())

    events, rest, _ = plan_backward()
    in_order = [e for key in sorted(events) for e in events[key]] + rest
    finals = [u for what, u, k in in_order if what == "p" and k == 4]

    chunk = D // dims[0]

    def upper(slot, h):
        return ws[slot, h].reshape(chunk, D)

    def side(it, j, which):
        return jnp.where(core == which, lax.rem(it * 8 + j, SLOTS), SLOTS + j % 2)

    def outer(index, left, right):
        for first in range(0, D, TILE):
            cols = slice(first, first + TILE)
            value = nn_dot(left[...], right[:, cols]).astype(HALF)
            stage[index, :, :, :, :, cols] = value.reshape(dims + (rank, TILE))

    def back(dst, terms, fresh, as_half=False):
        for h in range(dims[0]):
            cols = slice(h * chunk, (h + 1) * chunk)
            total = None
            for left, slot in terms:
                part = nt_dot(left[...], upper(slot, h))
                total = part if total is None else total + part
            if not fresh:
                total += dst[:, cols]
            dst[:, cols] = total.astype(HALF) if as_half else total

    def pair_free(it, j):
        if j >= 2:
            sib_send(it * 8 + j - 2, j % 2).wait_send()
        else:

            @pl.when(it > 0)
            def _():
                sib_send(it * 8 + j - 2, j % 2).wait_send()

    def emit(it, j):
        sib_send(it * 8 + j, j % 2).start()

    def norm_back(layer, j, last):
        gain = vec[layer, pl.ds(j, 1), :]
        load_xh(layer, j).wait()
        load_rstd(layer, j).wait()

        def body(i, carry):
            gains, total = carry
            rows = tile(i, ROWS)
            d = dx[rows, :]
            hat = xh[rows, :]
            dn = d * gain
            first = jnp.mean(dn, -1, keepdims=True)
            second = jnp.mean(dn * hat, -1, keepdims=True)
            out = g[rows, :] + rstd[rows, :][:, :1] * (dn - first - hat * second)
            g[rows, :] = out
            gb[rows, :] = out.astype(HALF)
            gains = gains + jnp.sum((d * hat).reshape(ROWS // 8, 8, D), 0)
            if last:
                dxb[rows, :] = out.astype(HALF)
                total = total + jnp.sum(out.reshape(ROWS // 8, 8, D), 0)
            return gains, total

        zero = jnp.zeros((8, D), FULL)
        gains, total = lax.fori_loop(0, SEQ // ROWS, body, (zero, zero))
        sm[0, layer, pl.ds(j, 1), :] = jnp.sum(gains, 0, keepdims=True)
        if last:
            whole = jnp.sum(total, 0, keepdims=True)
            sm[0, layer, pl.ds(3, 1), :] = jnp.where(kind == 1, 0.0, whole)
            sm[0, layer, pl.ds(4, 1), :] = jnp.where(kind == 1, whole, 0.0)

    def attend_back(layer, which, count, causal, point):
        def pair(hp):
            cols = tile(hp, 128)
            q2 = qkv[0, :, cols] * jnp.asarray(0.125, HALF)
            k2 = qkv[1, :, cols]
            v2 = qkv[2, :, cols]
            do2 = work[3, :, cols]
            kt = k2.T
            dk = [None, None]
            dv = [None, None]

            def put(acc, value, keys):
                for h in range(keys // TILE):
                    piece = value[h * TILE : (h + 1) * TILE]
                    acc[h] = piece if acc[h] is None else acc[h] + piece

            halves = [lane_half(0), lane_half(1)]
            ka, va, qa, da = [[m * half for half in halves] for m in (k2, v2, q2, do2)]
            keys = {f: f + TILE if causal else SEQ for f in range(0, SEQ, TILE)}
            rows = [[], []]
            for f in range(0, SEQ, TILE):
                scores, dps, probs, ds = {}, {}, {}, {}
                for a in range(2):
                    scores[a] = nt_dot(ka[a][: keys[f]], q2[f : f + TILE])
                    dps[a] = nt_dot(va[a][: keys[f]], do2[f : f + TILE])
                for a in range(2):
                    shift = lse[layer, which, hp, pl.ds(a, 1), pl.ds(f, TILE)]
                    p = jnp.exp(scores[a] - shift)
                    p = jnp.where(allowed(keys[f], f, count, causal), p, 0.0)
                    mix = jnp.sum(dps[a] * p, 0, keepdims=True)
                    ds[a] = (p * (dps[a] - mix)).astype(HALF)
                    probs[a] = p.astype(HALF)
                for a in range(2):
                    put(dv, nn_dot(probs[a], da[a][f : f + TILE]), keys[f])
                    put(dk, nn_dot(ds[a], qa[a][f : f + TILE]), keys[f])
                    rows[a].append(nn_dot(kt[a * 64 : a * 64 + 64, : keys[f]], ds[a]))
            dq = [jnp.concatenate(r, 1) for r in rows]
            whole = jnp.concatenate(dq, 0) * 0.125
            work[0, :, cols] = whole.T.astype(HALF)
            for h in range(SEQ // TILE):
                rows = pl.ds(h * TILE, TILE)
                work[1, rows, cols] = dk[h].astype(HALF)
                work[2, rows, cols] = dv[h].astype(HALF)

        for part_of in range(4):
            point()
            loop(HEADS // 8, lambda hp, part_of=part_of: pair(part_of * (HEADS // 8) + hp))

    def give(layer, src, dst, base):
        @pl.when(core == layer)
        def _():
            local(src, dst.at[mine], out_sem.at[base]).start()

        @pl.when(core != layer)
        def _():
            remote(
                src, dst.at[mine], out_sem.at[base + 1], out_sem.at[base + 2], place.twin()
            ).start()

    def given(layer, src, dst, base):
        @pl.when(core == layer)
        def _():
            local(src, dst.at[mine], out_sem.at[base]).wait()

        @pl.when(core != layer)
        def _():
            remote(
                src, dst.at[mine], out_sem.at[base + 1], out_sem.at[base + 2], place.twin()
            ).wait_send()

    def give_done(src, dst, base):
        given(0, src, dst, base)
        remote(
            src, dst.at[twins], out_sem.at[base + 1], out_sem.at[base + 2], place.twin()
        ).wait_recv()

    for slot, b in ((0, 12), (1, 8), (2, 13), (3, 9)):
        load_w(slot, 1, b).start()

    def layer_body(it):
        l = 1 - it
        passed = []

        def point():
            i = len(passed)
            passed.append(i)
            for turn in range(2):
                if events[turn, i]:

                    @pl.when(it == turn)
                    def _(turn=turn):
                        for event in events[turn, i]:
                            sum_event(*event)

        point()
        count_self = meta[0, core]
        count_cross = meta[2, core]

        @pl.when(it > 0)
        def _():
            given(1, deb, de_out, 3)

        @pl.when(core == l)
        def _():
            local(cot.at[mine], deb, cot_sem.at[0]).start()

        @pl.when(core != l)
        def _():
            remote(
                cot.at[mine], cot_land, cot_swap.at[0], cot_swap.at[1], place.twin()
            ).wait_recv()
            local(cot_land, deb, cot_sem.at[0]).start()

        for slot in range(2):
            load_dg(slot, l, slot).start()
        load_xt(0, l, 5).start()
        for q in range(2):
            load_act(1 + q, l, q).start()
        load_xt(3, l, 2).start()
        for i in range(3):
            load_six(i, l, 3 + i).start()
        load_xh(l, 2).start()
        load_rstd(l, 2).start()
        local(cot.at[mine], deb, cot_sem.at[0]).wait()

        def begin(i):
            rows = tile(i, ROWS)
            value = deb[rows, :].astype(FULL)
            value = value + jnp.where(it > 0, g[rows, :].astype(HALF).astype(FULL), 0.0)
            g[rows, :] = value
            gb[rows, :] = value.astype(HALF)

        loop(SEQ // ROWS, begin)

        for q in range(4):
            pair = 2 * (q % 2)
            point()
            load_w(pair, l, 12 + q).wait()
            load_dg(q % 2, l, q).wait()

            for h in range(dims[0]):
                cols = slice(h * chunk, (h + 1) * chunk)
                d = nt_dot(gb[...], upper(pair, h))
                work[3, :, cols] = (d * work[q % 2, :, cols].astype(FULL)).astype(HALF)
            load_act(1 + q % 2, l, q).wait()
            point()
            pair_free(it, q)
            outer(side(it, q, 0), xtb.at[1 + q % 2], gb)
            point()
            if q == 0:
                load_xt(0, l, 5).wait()
            outer(side(it, q, 1), xtb.at[0], work.at[3])
            emit(it, q)
            point()
            load_w(pair + 1, l, 8 + q).wait()
            back(dx, [(work.at[3], pair + 1)], q == 0)
            if q < 2:
                load_w(pair, l, 14 + q).start()
                load_w(pair + 1, l, 10 + q).start()
                load_dg(q, l, q + 2).start()
                load_act(1 + q, l, q + 2).start()
            elif q == 2:
                load_w(0, l, 7).start()
                load_w(1, l, 6).start()
                load_xt(1, l, 4).start()
            else:
                load_w(2, l, 4).start()
                load_w(3, l, 5).start()
                load_xt(2, l, 3).start()
                load_xt(0, l, 1).start()
        point()
        norm_back(l, 2, False)
        load_xh(l, 1).start()
        load_rstd(l, 1).start()

        load_w(0, l, 7).wait()
        back(work.at[3], [(gb, 0)], True, True)
        load_w(0, l, 3).start()
        for i in range(3):
            load_six(i, l, 3 + i).wait()
        attend_back(l, 1, count_cross, False, point)
        for i in range(3):
            load_six(i, l, i).start()
        point()
        pair_free(it, 4)
        load_xt(3, l, 2).wait()
        outer(side(it, 4, 0), xtb.at[3], work.at[1])
        point()
        outer(side(it, 4, 1), xtb.at[3], work.at[2])
        load_xt(3, l, 0).start()
        emit(it, 4)
        point()
        load_w(2, l, 4).wait()
        load_w(3, l, 5).wait()
        back(deb, [(work.at[1], 2), (work.at[2], 3)], True, True)
        load_w(2, l, 0).start()
        load_w(3, l, 1).start()
        give(l, deb, de_out, 3)
        point()
        pair_free(it, 5)
        load_xt(1, l, 4).wait()
        outer(side(it, 5, 0), xtb.at[1], gb)
        point()
        load_xt(2, l, 3).wait()
        outer(side(it, 5, 1), xtb.at[2], work.at[0])
        emit(it, 5)
        point()
        load_w(1, l, 6).wait()
        back(dx, [(work.at[0], 1)], True)
        load_w(1, l, 2).start()
        norm_back(l, 1, False)
        load_xh(l, 0).start()
        load_rstd(l, 0).start()

        load_w(0, l, 3).wait()
        back(work.at[3], [(gb, 0)], True, True)

        @pl.when(it == 0)
        def _():
            load_w(0, 0, 12).start()

        for i in range(3):
            load_six(i, l, i).wait()
        attend_back(l, 0, count_self, True, point)
        point()
        pair_free(it, 6)
        load_xt(0, l, 1).wait()
        outer(side(it, 6, 0), xtb.at[0], gb)
        point()
        load_xt(3, l, 0).wait()
        outer(side(it, 6, 1), xtb.at[3], work.at[0])
        emit(it, 6)
        point()
        pair_free(it, 7)
        outer(side(it, 7, 0), xtb.at[3], work.at[1])
        point()
        outer(side(it, 7, 1), xtb.at[3], work.at[2])
        emit(it, 7)
        point()
        load_w(1, l, 2).wait()
        load_w(2, l, 0).wait()
        load_w(3, l, 1).wait()
        back(dx, [(work.at[0], 2), (work.at[1], 3), (work.at[2], 1)], True)

        @pl.when(it == 0)
        def _():
            load_w(1, 0, 8).start()
            load_w(2, 0, 13).start()
            load_w(3, 0, 9).start()

        @pl.when(it > 0)
        def _():
            given(1, dxb, dx_out, 0)

        norm_back(l, 0, True)
        give(l, dxb, dx_out, 0)
        assert len(passed) == len(BACKWARD_CHUNKS)

    tmp_z[...] = jnp.zeros(tmp_z.shape, HALF)
    loop(2, layer_body)

    axes = (2, 1, 0)

    def small_hop(k, step, base):
        return remote(
            sm.at[k + 1],
            sm_land.at[base],
            small_send.at[base],
            small_recv.at[base],
            place.peer(axes[k], step),
        )

    def small_twin():
        return remote(sm.at[0], sm_land.at[0], small_send.at[0], small_recv.at[0], place.twin())

    def bases(k):
        first = 1
        for axis in axes[:k]:
            first += dims[axis] - 1
        return [(step, first + step - 1) for step in range(1, dims[axes[k]])]

    def small_event(k):
        if k == 0:
            small_twin().start()
            return
        if k == 1:
            small_twin().wait_recv()
            sm[1] = sm[0] + sm_land[0]
        else:
            value = sm[k - 1]
            for step, base in bases(k - 2):
                small_hop(k - 2, step, base).wait_recv()
                value += sm_land[base]
            if k == 4:
                small_out[...] = value
                return
            sm[k] = value
        for step, base in bases(k - 1):
            small_hop(k - 1, step, base).start()

    every = max(1, len(rest) // 5)
    for e in range(5):
        small_event(e)
        for event in rest[e * every : (e + 1) * every if e < 4 else None]:
            sum_event(*event)

    small_twin().wait_send()
    for k in range(3):
        for step, base in bases(k):
            small_hop(k, step, base).wait_send()
    cot_send.wait_send()
    for u in (14, 15):
        sib_send(u, u % 2).wait_send()
    for u in finals[-2:]:
        fin_wait(u)
    for j in range(8):
        unit = (1 - core) * 8 + j
        remote(
            fin.at[j % 2],
            grad_out.at[twin_block(j)],
            fin_send.at[unit],
            fin_recv.at[unit],
            place.twin(),
        ).wait_recv()
    give_done(dxb, dx_out, 0)
    give_done(deb, de_out, 3)


def run_backward(dims, meta, cot, w_all, saved):
    rank = D // (dims[0] * dims[1] * dims[2])
    anyw = pl.BlockSpec(memory_space=pl.ANY)
    vmem = pl.BlockSpec(memory_space=pltpu.VMEM)
    wide = max(dims[1:])
    smalls = 1 + sum(size - 1 for size in dims)
    dma = pltpu.SemaphoreType.DMA
    shape = jax.ShapeDtypeStruct
    return pl.pallas_call(
        functools.partial(backward_kernel, dims),
        out_shape=(
            shape((2 * SEQ, D), HALF),
            shape((2 * SEQ, D), HALF),
            shape((16, rank, D), FULL),
            shape((2, 8, D), FULL),
            shape((SEQ, D), HALF),
            shape((16,) + dims + (rank, D), HALF),
            shape((16, wide - 1, dims[0], wide, rank, D), HALF),
            shape((16, wide - 1, dims[0], rank, D), HALF),
            shape((16, DEEP_SLOTS, wide, rank, D), HALF),
        ),
        in_specs=[pl.BlockSpec(memory_space=pltpu.SMEM)] + [anyw] * 8 + [vmem] * 2,
        out_specs=(anyw, anyw, anyw, vmem) + (anyw,) * 5,
        scratch_shapes=[
            pltpu.VMEM((SLOTS + 2,) + dims + (rank, D), HALF),
            pltpu.VMEM((4,) + dims + (rank, D), HALF),
            pltpu.VMEM((SEQ, D), FULL),
            pltpu.VMEM((SEQ, D), FULL),
            pltpu.VMEM((SEQ, D), HALF),
            pltpu.VMEM((3, SEQ, D), HALF),
            pltpu.VMEM((4, SEQ, D), HALF),
            pltpu.VMEM((4, D, SEQ), HALF),
            pltpu.VMEM((SEQ, D), FULL),
            pltpu.VMEM((SEQ, 128), FULL),
            pltpu.VMEM(dims + (rank, D), HALF),
            pltpu.VMEM((wide - 1, dims[0], wide, rank, D), HALF),
            pltpu.VMEM((DEEP_SLOTS, wide, rank, D), HALF),
            pltpu.VMEM((SEQ, D), HALF),
            pltpu.VMEM((SEQ, D), HALF),
            pltpu.VMEM((2, rank, D), FULL),
            pltpu.VMEM((4, 2, 8, D), FULL),
            pltpu.VMEM((smalls, 2, 8, D), FULL),
            dma((4,)),
            dma((3,)),
            dma((4,)),
            dma((2,)),
            dma((2,)),
            dma((1,)),
            dma((2,)),
            dma((16,)),
            dma((16,)),
            dma((16, 3, DEEP_SLOTS)),
            dma((16, 3, DEEP_SLOTS)),
            dma((4, DEEP_SLOTS)),
            dma((2,)),
            dma((16,)),
            dma((16,)),
            dma((6,)),
            dma((smalls,)),
            dma((smalls,)),
        ],
        compiler_params=pltpu.CompilerParams(
            collective_id=1, has_side_effects=True, vmem_limit_bytes=62 * 2**20
        ),
        cost_estimate=pl.CostEstimate(
            flops=80 * 10**9, bytes_accessed=4 * 10**8, transcendentals=10**7
        ),
    )(meta, cot, w_all, *saved)


def per_device(
    inputs,
    qkv_weight,
    out_weight,
    cross_query,
    cross_kv,
    cross_out,
    ffn_in,
    ffn_out,
    norm_gains,
    type_embed,
    encoder,
    lengths,
    seq_types,
    enc_mask,
    cotangent,
):
    chips = lax.axis_size("dp")
    dims = grid_of(chips)
    rank = D // chips
    pack = packed(
        qkv_weight, out_weight, cross_query, cross_kv, cross_out, ffn_in, ffn_out, chips
    )
    small = small_block(norm_gains, type_embed)
    meta = jnp.stack([lengths, seq_types, jnp.sum(enc_mask, 1)])
    w_all, outs, *saved = run_forward(dims, meta, pack, small, inputs, encoder[0])
    grads = run_backward(dims, meta, cotangent[0], w_all, saved)
    d_in, d_mem, blocks, sums = grads[:4]

    def columns(first, last):
        return jnp.moveaxis(blocks[first:last], 0, 1).reshape(1, rank, -1)

    inner = blocks[8:12].reshape(4, rank, chips, rank).transpose(1, 2, 0, 3)
    own = lax.dynamic_index_in_dim(sums, lax.axis_index("section"), 0, keepdims=False)
    own = lax.dynamic_slice_in_dim(own, lax.axis_index("dp") * rank, rank, 1)
    return (
        outs[None],
        d_in[None],
        d_mem[None],
        columns(0, 3),
        blocks[3:4],
        blocks[6:7],
        columns(4, 6),
        blocks[7:8],
        inner.reshape(1, rank, 4 * D),
        blocks[12:16].reshape(1, 4 * rank, D),
        own[None, :3],
        own[None, 3:5],
    )


def solution(mesh):
    rows = P("section", "dp", None)
    cols = P("section", None, "dp")
    in_specs = (
        (P("dp", None),)
        + (rows,) * 7
        + (cols, cols, rows, P("dp"), P("dp"), P("dp", None), rows)
    )
    out_specs = (rows,) * 10 + (cols, cols)
    return jax.shard_map(
        per_device, mesh=mesh, in_specs=in_specs, out_specs=out_specs, check_vma=False
    )
```

```python
import functools

import jax
import jax.numpy as jnp
from jax import lax
from jax.experimental import pallas as pl
from jax.experimental.pallas import tpu as pltpu
from jax.sharding import PartitionSpec as P

D = 1024
HEADS = 16
SEQ = 512
EPS = 1e-05
NEG = -1e30
MESH = pl.DeviceIdType.MESH
HALF = jnp.bfloat16
FULL = jnp.float32
TILE = 256
ROWS = 128


def grid_of(n):
    deep = 4 if n % 4 == 0 else 1
    rest = n // deep
    wide = max(k for k in range(1, rest + 1) if rest % k == 0 and k * k <= rest)
    return (deep, wide, rest // wide)


class Place:
    def __init__(self, dims):
        self.dims = dims
        self.chip = lax.axis_index("dp")
        self.core = lax.axis_index("section")
        self.other = 1 - self.core
        deep, wide, long = dims
        self.at = (
            self.chip // (wide * long),
            lax.rem(self.chip // long, wide),
            lax.rem(self.chip, long),
        )

    def shifted(self, axis, step):
        where = list(self.at)
        where[axis] = lax.rem(self.at[axis] + step + self.dims[axis], self.dims[axis])
        return where

    def peer(self, axis, step):
        where = self.shifted(axis, step)
        return (self.core, (where[0] * self.dims[1] + where[1]) * self.dims[2] + where[2])

    def twin(self):
        return (self.other, self.chip)

    def greet(self):
        barrier = pltpu.get_barrier_semaphore()
        peers = [self.peer(a, s) for a in range(3) for s in range(1, self.dims[a])]
        peers.append(self.twin())
        for peer in peers:
            pl.semaphore_signal(barrier, inc=1, device_id=peer, device_id_type=MESH)
        pl.semaphore_wait(barrier, len(peers))


def remote(src, dst, send, recv, peer):
    return pltpu.make_async_remote_copy(
        src_ref=src, dst_ref=dst, send_sem=send, recv_sem=recv, device_id=peer, device_id_type=MESH
    )


def local(src, dst, sem):
    return pltpu.make_async_copy(src, dst, sem)


def nt_dot(left, right):
    return lax.dot_general(
        left, right, (((1,), (1,)), ((), ())), preferred_element_type=FULL
    )


def nn_dot(left, right):
    return jnp.dot(left, right, preferred_element_type=FULL)


def tile(i, size=TILE):
    return pl.ds(pl.multiple_of(i * size, size), size)


def loop(count, body):
    def step(i, carry):
        body(i)
        return carry

    lax.fori_loop(0, count, step, 0)


def lane_half(a):
    lane = lax.broadcasted_iota(jnp.int32, (1, 128), 1)
    return jnp.where((lane // 64) == a, 1.0, 0.0).astype(HALF)


def allowed(keys, first, count, causal):
    key = lax.broadcasted_iota(jnp.int32, (keys, TILE), 0)
    ok = key < count
    if causal:
        ok = ok & (key <= first + lax.broadcasted_iota(jnp.int32, (keys, TILE), 1))
    return ok


ORDER_A = (0, 2, 1)
ORDER_B = (0, 1, 2)
ORDER_C = (2, 0, 1)
ORDER_D = (1, 0, 2)
DEEP_SLOTS = 5
GATHER_MARGIN = 3.0
SUM_MARGIN = 0.0


def deep_sends(k):
    if k == 0:
        return [
            (0, lambda z: z < 3, 1),
            (1, lambda z: z > 0, -1),
            (2, lambda z: z < 2, 2),
            (3, lambda z: z > 1, -2),
        ]
    return [(4, lambda z: z == 2, 1), (4, lambda z: z == 1, -1)]


def stages_of(order):
    found = []
    for axis in order:
        found += [(axis, 0), (axis, 1)] if axis == 0 else [(axis, 0)]
    return found


class Plan:
    UNIT = 2.85
    LATENCY = 2.0

    def __init__(self):
        self.free = {}
        self.time = 0.0
        self.queue = []
        self.count = 0

    def push(self, ready, event):
        self.queue.append((ready, self.count, event))
        self.count += 1

    def occupy(self, loads):
        end = self.time
        for link, load in loads:
            begin = max(self.time, self.free.get(link, 0.0))
            self.free[link] = begin + load
            end = max(end, begin + load)
        return end + self.LATENCY

    def pop(self, before, allowed=lambda event: True):
        ready = [item for item in self.queue if item[0] <= before and allowed(item[2])]
        if not ready:
            return None
        item = min(ready)
        self.queue.remove(item)
        self.time = max(self.time, item[0])
        return item[2]


def stage_loads(order, k, gather):
    stages = stages_of(order)
    axis, part = stages[k]
    size = (4, 2, 2)
    if gather:
        held = 1
        for other in set(a for a, _ in stages[:k]):
            if other != axis:
                held *= size[other]
    else:
        held = 16
        for other in set(a for a, _ in stages[: k + 1]):
            held //= size[other]
    if axis != 0:
        return [(axis, held * Plan.UNIT)]
    far, near = ("middle", "end") if gather else ("end", "middle")
    if part == 0:
        return [(far, 3 * held * Plan.UNIT), (near, 2 * held * Plan.UNIT)]
    return [(near, held * Plan.UNIT)]


FORWARD_CHUNKS = (
    [(4, None), (2, 0), (1.5, 0), (1.5, 0)] + [(2, 0)] * 4 + [(2, 0), (4, None)]
    + [(2.5, 1), (1.5, 1), (1.5, 1)] + [(2, 1)] * 4 + [(2, 1), (3, None)]
    + [(4, 2)] + [(3.5, 2)] * 3 + [(7, 3)]
)
GATHER_ORDERS = (
    ORDER_A, ORDER_B, ORDER_C, ORDER_D, ORDER_A, ORDER_B, ORDER_C, ORDER_D,
    ORDER_A, ORDER_B, ORDER_C, ORDER_D, ORDER_A, ORDER_B, ORDER_C, ORDER_D,
)
GATHER_WINDOW = 3
GATHER_STAGE = 2


def plan_forward():
    plan = Plan()
    after = {}
    for u in range(GATHER_WINDOW):
        plan.push(0.0, (u, 0))
    following = GATHER_WINDOW
    plan.push(0.0, (-1, 0))
    done = set()

    def take(event, out):
        nonlocal following
        u, k = event
        plan.time += 0.4
        done.add(event)
        out.append(event)
        if u < 0:
            if k < 4:
                plan.push(plan.time + 3.0, (u, k + 1))
            return
        if k < 4:
            loads = stage_loads(GATHER_ORDERS[u], k, True)
            plan.push(plan.occupy(loads), (u, k + 1))
        elif k == 4:
            plan.push(plan.occupy([("twin", 4.0)]), (u, 5))
        if k == GATHER_STAGE and following < 16:
            plan.push(plan.time, (following, 0))
            following += 1

    for layer in range(2):
        for i, (length, group) in enumerate(FORWARD_CHUNKS):
            out = []
            while True:
                event = plan.pop(plan.time - GATHER_MARGIN)
                if event is None:
                    break
                take(event, out)
            need = [(-1, 4)]
            if group is not None:
                first = 2 * (4 * layer + group)
                need += [(first, 5), (first + 1, 5)]
            while not done.issuperset(need):
                take(plan.pop(1e9), out)
            plan.time += length
            after[layer, i] = out
    assert not plan.queue and following == 16
    return after, plan.time


def forward_kernel(
    dims,
    meta,
    pack,
    small,
    hidden,
    frames,
    w_all,
    y_out,
    six_out,
    xt_out,
    actt_out,
    dg_out,
    xh_out,
    rstd_out,
    lse_out,
    vec_out,
    ws,
    res,
    xb,
    mem,
    six,
    xt,
    actn,
    actt,
    dg,
    xh,
    hin,
    yb,
    vecs,
    seed_sem,
    swap_send,
    swap_recv,
    hop_send,
    hop_recv,
    twin_send,
    twin_recv,
    vec_send,
    vec_recv,
    vec_swap,
    in_sem,
    frame_sem,
    y_sem,
    w_sem,
    save_sem,
):
    place = Place(dims)
    core, other, at = place.core, place.other, place.at
    place.greet()

    def seed(g):
        return local(
            pack.at[g, pl.ds(2 * core, 2)],
            w_all.at[pl.ds((core * 4 + g) * 4 + 2 * core, 2), at[0], at[1], at[2]],
            seed_sem.at[g],
        )

    def swap(g):
        return remote(
            pack.at[g, pl.ds(2 * other, 2)],
            w_all.at[pl.ds((core * 4 + g) * 4 + 2 * other, 2), at[0], at[1], at[2]],
            swap_send.at[g],
            swap_recv.at[g],
            place.twin(),
        )

    def swapped(layer, g):
        spot = w_all.at[pl.ds((layer * 4 + g) * 4 + 2 * core, 2), at[0], at[1], at[2]]
        return remote(spot, spot, swap_send.at[g], swap_recv.at[g], place.twin())

    own_vec = vecs.at[core, at[0], at[1], at[2]]
    vec_in = local(small, own_vec, in_sem.at[0])
    vec_in.start()
    mine = pl.ds(core * SEQ, SEQ)
    twins = pl.ds(other * SEQ, SEQ)
    hid_in = local(hidden.at[mine], hin, in_sem.at[1])
    hid_in.start()
    mem_in = local(frames.at[mine], mem.at[core], in_sem.at[2])
    mem_in.start()
    for g in range(4):
        seed(g).start()
        swap(g).start()
    mem_swap = remote(
        frames.at[twins], mem.at[core], frame_sem.at[0], frame_sem.at[1], place.twin()
    )
    mem_swap.start()

    def block_of(u):
        return (u // 2) * 4 + 2 * core + u % 2

    def part(order, k, place_of):
        axis = stages_of(order)[k][0]
        index = []
        for other_axis in range(3):
            if other_axis == axis:
                index.append(place_of)
            elif other_axis in [a for a, _ in stages_of(order)[:k]]:
                index.append(slice(None))
            else:
                index.append(at[other_axis])
        return tuple(index)

    def stage_copies(order, k, base, prefix, send, recv, sending):
        axis, piece = stages_of(order)[k]
        found = []
        if axis != 0:
            for step in range(1, dims[axis]):
                where = place.shifted(axis, 0 if sending else -step)[axis]
                ref = base.at[prefix + part(order, k, where)]
                sems = (send.at[axis, step - 1], recv.at[axis, step - 1])
                found.append((None, remote(ref, ref, *sems, place.peer(axis, step))))
            return found
        if dims[0] == 1:
            return found
        for slot, test, step in deep_sends(piece):
            sems = (send.at[0, slot], recv.at[0, slot])
            if sending:
                from_z = at[0] if piece == 0 else (0 if step > 0 else dims[0] - 1)
                okay = test(at[0])
            else:
                from_z = at[0] - step if piece == 0 else (0 if step > 0 else dims[0] - 1)
                okay = test(at[0] - step) & (at[0] - step >= 0) & (at[0] - step < dims[0])
                from_z = jnp.clip(from_z, 0, dims[0] - 1)
            ref = base.at[prefix + part(order, k, from_z)]
            found.append((okay, remote(ref, ref, *sems, place.peer(0, step))))
        return found

    def each(copies, act):
        for okay, copy in copies:
            if okay is None:
                act(copy)
            else:
                pl.when(okay)(functools.partial(act, copy))

    def hops_of(u, k, sending):
        return stage_copies(
            GATHER_ORDERS[u], k, w_all, (block_of(u),), hop_send.at[u], hop_recv.at[u], sending
        )

    def vec_hops(k, sending):
        return stage_copies(ORDER_B, k, vecs, (core,), vec_send, vec_recv, sending)

    def twin_copy(u, block):
        return remote(
            w_all.at[block], w_all.at[block], twin_send.at[u], twin_recv.at[u], place.twin()
        )

    def vec_twin(layer):
        return remote(
            vecs.at[layer], vecs.at[layer], vec_swap.at[0], vec_swap.at[1], place.twin()
        )

    def event(u, k):
        if u < 0:
            if k == 0:
                vec_in.wait()
            else:
                each(vec_hops(k - 1, False), lambda copy: copy.wait_recv())
            if k < 4:
                each(vec_hops(k, True), lambda copy: copy.start())
            else:
                vec_twin(core).start()
                vec_twin(other).wait_recv()
            return
        layer, g = u // 8, (u // 2) % 4
        if k == 0 and u % 2 == 0:

            @pl.when(core == layer)
            def _():
                seed(g).wait()

            @pl.when(core != layer)
            def _():
                swapped(layer, g).wait_recv()

        if 0 < k <= 4:
            each(hops_of(u, k - 1, False), lambda copy: copy.wait_recv())
        if k < 4:
            each(hops_of(u, k, True), lambda copy: copy.start())
        elif k == 4:
            twin_copy(u, block_of(u)).start()
        else:
            twin_copy(u, (u // 2) * 4 + 2 * other + u % 2).wait_recv()

    events, _ = plan_forward()

    def save_to(layer, kind, i):
        src, dst, first = {
            "six": (six, six_out, 0),
            "xt": (xt, xt_out, 6),
            "actt": (actt, actt_out, 12),
            "dg": (dg, dg_out, 16),
            "xh": (xh, xh_out, 20),
        }[kind]
        return local(src.at[i], dst.at[layer, i], save_sem.at[first + i])

    saves = (
        [("six", i) for i in range(6)]
        + [("xt", i) for i in range(6)]
        + [("actt", i) for i in range(4)]
        + [("dg", i) for i in range(4)]
        + [("xh", i) for i in range(3)]
    )

    def weight(s, cols=slice(None)):
        block = ws[s, :, :, :, :, cols]
        return block.reshape(D, block.shape[-1])

    def early():
        hid_in.wait()
        mem_in.wait()
        remote(
            frames.at[mine], mem.at[other], frame_sem.at[0], frame_sem.at[1], place.twin()
        ).wait_recv()

    count_self = meta[0, core]
    kind = meta[1, core]
    count_cross = meta[2, core]

    def layer_body(l):
        def guard(what, i):
            @pl.when(l > 0)
            def _():
                save_to(l - 1, what, i).wait()

        def save(what, i):
            save_to(l, what, i).start()

        passed = []

        def point():
            i = len(passed)
            passed.append(i)
            for layer in range(2):
                if events[layer, i]:

                    @pl.when(l == layer)
                    def _(layer=layer):
                        for u, k in events[layer, i]:
                            event(u, k)

        def fetch(g):
            for q in range(4):
                local(w_all.at[(l * 4 + g) * 4 + q], ws.at[q], w_sem.at[q]).start()

        def ready(g, q):
            local(w_all.at[(l * 4 + g) * 4 + q], ws.at[q], w_sem.at[q]).wait()

        def flip(src, i):
            guard("xt", i)

            def step(n):
                xt[i, tile(n), :] = src[:, tile(n)].T

            loop(D // TILE, step)
            save("xt", i)

        def norm(j):
            gain = vec_out[l, pl.ds(j, 1), :]
            guard("xh", j)

            def step(i):
                rows = tile(i, ROWS)
                v = res[rows, :]
                cent = v - jnp.mean(v, -1, keepdims=True)
                rstd = lax.rsqrt(jnp.mean(cent * cent, -1, keepdims=True) + EPS)
                hat = cent * rstd
                xh[j, rows, :] = hat
                rstd_out[l, j, rows, :] = jnp.broadcast_to(rstd, (ROWS, 128))
                xb[rows, :] = (hat * gain).astype(HALF)

            loop(SEQ // ROWS, step)
            save("xh", j)

        def project(src, s, i):
            guard("six", i)

            six[i] = nn_dot(src[...], weight(s)).astype(HALF)
            save("six", i)

        def attend(qi, ki, vi, which, out, count, causal):
            guard("xt", out)

            def pair(hp):
                cols = tile(hp, 128)
                q2 = six[qi, :, cols] * jnp.asarray(0.125, HALF)
                k2 = six[ki, :, cols]
                vt = six[vi, :, cols].T
                ka = [k2 * lane_half(a) for a in range(2)]
                for f in range(0, SEQ, TILE):
                    keys = f + TILE if causal else SEQ
                    scores = [nt_dot(ka[a][:keys], q2[f : f + TILE]) for a in range(2)]
                    probs = []
                    for a in range(2):
                        s = jnp.where(allowed(keys, f, count, causal), scores[a], NEG)
                        top = jnp.max(s, 0, keepdims=True)
                        expo = jnp.exp(s - top)
                        total = jnp.sum(expo, 0, keepdims=True)
                        probs.append((expo * (1.0 / total)).astype(HALF))
                        lse_out[l, which, hp, pl.ds(a, 1), pl.ds(f, TILE)] = top + jnp.log(total)
                    for a in range(2):
                        o = nn_dot(vt[a * 64 : a * 64 + 64, :keys], probs[a])
                        xt[out, pl.ds(hp * 128 + a * 64, 64), pl.ds(f, TILE)] = o.astype(HALF)
                xb[:, cols] = xt[out, tile(hp, 128), :].T

            for part_of in range(4):
                if part_of:
                    point()
                loop(HEADS // 8, lambda hp, part_of=part_of: pair(part_of * (HEADS // 8) + hp))
            save("xt", out)

        def add_product(src, s):
            res[...] += nn_dot(src[...], weight(s))

        point()

        @pl.when(l == 0)
        def _():
            early()
            rank = D // (dims[0] * dims[1] * dims[2])
            vec_out[...] = jnp.zeros(vec_out.shape, FULL)

            def step(j):
                row = lax.broadcasted_iota(jnp.int32, (128, D), 0)
                col = lax.broadcasted_iota(jnp.int32, (128, D), 1)
                spread = jnp.where((col == j * rank + row) & (row < rank), 1.0, 0.0).astype(HALF)
                z = j // (dims[1] * dims[2])
                y = lax.rem(j // dims[2], dims[1])
                x = lax.rem(j, dims[2])
                for m in range(2):
                    vec_out[m] += nn_dot(vecs[m, z, y, x], spread)

            loop(dims[0] * dims[1] * dims[2], step)

        shift = jnp.where(kind == 1, vec_out[l, pl.ds(4, 1), :], vec_out[l, pl.ds(3, 1), :])

        def begin(i):
            rows = tile(i, ROWS)
            came = jnp.where(l == 0, hin[rows, :].astype(FULL), yb[0, rows, :].astype(FULL))
            res[rows, :] = came + shift

        loop(SEQ // ROWS, begin)
        norm(0)
        flip(xb, 0)
        point()
        fetch(0)
        for q in range(3):
            if q:
                point()
            ready(0, q)
            project(xb, q, q)
        point()
        attend(0, 1, 2, 0, 1, count_self, True)
        point()
        ready(0, 3)
        add_product(xb, 3)
        point()
        norm(1)
        flip(xb, 3)
        flip(mem.at[l], 2)
        point()
        fetch(1)
        ready(1, 2)
        project(xb, 2, 3)
        point()
        ready(1, 0)
        project(mem.at[l], 0, 4)
        point()
        ready(1, 1)
        project(mem.at[l], 1, 5)
        point()
        attend(3, 4, 5, 1, 4, count_cross, False)
        point()
        ready(1, 3)
        add_product(xb, 3)
        point()
        norm(2)
        flip(xb, 5)
        for q in range(4):
            point()
            if q == 0:
                fetch(2)
            ready(2, q)
            guard("dg", q)
            guard("actt", q)

            for first in range(0, D, 512):
                cols = slice(first, first + 512)
                u = nn_dot(xb[...], weight(q, cols))
                cdf = 0.5 * (1.0 + lax.erf(u * (0.5**0.5)))
                act = (u * cdf).astype(HALF)
                actn[q, :, cols] = act
                actt[q, cols, :] = act.T
                bell = jnp.exp(-0.5 * u * u) * 0.3989422804014327
                dg[q, :, cols] = (cdf + u * bell).astype(HALF)
            save("dg", q)
            save("actt", q)
        point()
        fetch(3)
        for q in range(4):
            ready(3, q)
        assert len(passed) == len(FORWARD_CHUNKS)

        for first in range(0, D, 512):
            cols = slice(first, first + 512)
            total = res[:, cols]
            for q in range(4):
                total += nn_dot(actn[q], weight(q, cols))
            yb[l, :, cols] = total.astype(HALF)

        @pl.when(core == l)
        def _():
            local(yb.at[l], y_out.at[mine], y_sem.at[0]).start()

        @pl.when(core != l)
        def _():
            remote(yb.at[l], y_out.at[mine], y_sem.at[1], y_sem.at[2], place.twin()).start()

    loop(2, layer_body)

    for what, i in saves:
        save_to(1, what, i).wait()
    local(yb.at[core], y_out.at[mine], y_sem.at[0]).wait()
    remote(yb.at[other], y_out.at[mine], y_sem.at[1], y_sem.at[2], place.twin()).wait_send()
    remote(yb.at[core], y_out.at[twins], y_sem.at[1], y_sem.at[2], place.twin()).wait_recv()
    mem_swap.wait_send()
    for g in range(4):
        swap(g).wait_send()
    for k in range(4):
        each(vec_hops(k, True), lambda copy: copy.wait_send())
    vec_twin(core).wait_send()
    for u in range(16):
        for k in range(4):
            each(hops_of(u, k, True), lambda copy: copy.wait_send())
        twin_copy(u, block_of(u)).wait_send()


def run_forward(dims, meta, pack, small, hidden, frames):
    rank = D // (dims[0] * dims[1] * dims[2])
    anyw = pl.BlockSpec(memory_space=pl.ANY)
    vmem = pl.BlockSpec(memory_space=pltpu.VMEM)
    dma = pltpu.SemaphoreType.DMA
    shape = jax.ShapeDtypeStruct
    return pl.pallas_call(
        functools.partial(forward_kernel, dims),
        out_shape=(
            shape((32,) + dims + (rank, D), HALF),
            shape((2 * SEQ, D), HALF),
            shape((2, 6, SEQ, D), HALF),
            shape((2, 6, D, SEQ), HALF),
            shape((2, 4, D, SEQ), HALF),
            shape((2, 4, SEQ, D), HALF),
            shape((2, 3, SEQ, D), FULL),
            shape((2, 3, SEQ, 128), FULL),
            shape((2, 2, HEADS // 2, 2, SEQ), FULL),
            shape((2, 16, D), FULL),
        ),
        in_specs=[pl.BlockSpec(memory_space=pltpu.SMEM), vmem] + [anyw] * 3,
        out_specs=(anyw,) * 7 + (vmem,) * 3,
        scratch_shapes=[
            pltpu.VMEM((4,) + dims + (rank, D), HALF),
            pltpu.VMEM((SEQ, D), FULL),
            pltpu.VMEM((SEQ, D), HALF),
            pltpu.VMEM((2, SEQ, D), HALF),
            pltpu.VMEM((6, SEQ, D), HALF),
            pltpu.VMEM((6, D, SEQ), HALF),
            pltpu.VMEM((4, SEQ, D), HALF),
            pltpu.VMEM((4, D, SEQ), HALF),
            pltpu.VMEM((4, SEQ, D), HALF),
            pltpu.VMEM((3, SEQ, D), FULL),
            pltpu.VMEM((SEQ, D), HALF),
            pltpu.VMEM((2, SEQ, D), HALF),
            pltpu.VMEM((2,) + dims + (16, 128), HALF),
            dma((4,)),
            dma((4,)),
            dma((4,)),
            dma((16, 3, DEEP_SLOTS)),
            dma((16, 3, DEEP_SLOTS)),
            dma((16,)),
            dma((16,)),
            dma((3, DEEP_SLOTS)),
            dma((3, DEEP_SLOTS)),
            dma((2,)),
            dma((3,)),
            dma((2,)),
            dma((3,)),
            dma((4,)),
            dma((23,)),
        ],
        compiler_params=pltpu.CompilerParams(
            collective_id=0, has_side_effects=True, vmem_limit_bytes=60 * 2**20
        ),
        cost_estimate=pl.CostEstimate(
            flops=40 * 10**9, bytes_accessed=3 * 10**8, transcendentals=10**7
        ),
    )(meta, pack, small, hidden, frames)


def packed(qkv_weight, out_weight, cross_query, cross_kv, cross_out, ffn_in, ffn_out, chips):
    rank = qkv_weight.shape[1]

    def columns(w):
        return jnp.moveaxis(w[0].astype(HALF).reshape(rank, -1, D), 1, 0)

    inner = ffn_in[0].astype(HALF).reshape(rank, chips, 4, rank)
    inner = inner.transpose(2, 0, 1, 3).reshape(4, rank, D)
    outer = ffn_out[0].astype(HALF).reshape(4, rank, D)
    first = jnp.concatenate([columns(qkv_weight), columns(out_weight)], 0)
    second = jnp.concatenate([columns(cross_kv), columns(cross_query), columns(cross_out)], 0)
    return jnp.stack([first, second, inner, outer])


def small_block(norm_gains, type_embed):
    rows = jnp.concatenate([norm_gains[0], type_embed[0]], 0).astype(HALF)
    return jnp.pad(rows, ((0, 16 - rows.shape[0]), (0, 128 - rows.shape[1])))


SUM_A = (1, 2, 0)
SUM_B = (2, 1, 0)
SUM_C = (1, 0, 2)
SUM_D = (2, 0, 1)
SUM_ORDERS = (
    SUM_C, SUM_B, SUM_C, SUM_B, SUM_D, SUM_A, SUM_C, SUM_B,
    SUM_D, SUM_B, SUM_C, SUM_C, SUM_B, SUM_D, SUM_C, SUM_B,
)
SLOTS = 7
PAIRS = ((12, 8), (13, 9), (14, 10), (15, 11), (4, 5), (7, 6), (3, 0), (1, 2))


def deep_sums(k):
    if k == 0:
        return [
            (0, lambda z: z < 3, lambda z: z + 1, 1),
            (1, lambda z: z > 0, lambda z: z - 1, -1),
            (2, lambda z: z == 0, lambda z: 2, 2),
            (3, lambda z: z == 3, lambda z: 1, -2),
            (4, lambda z: z == 0, lambda z: 3, 1),
            (4, lambda z: z == 3, lambda z: 0, -1),
        ]
    return [(2, lambda z: z == 1, lambda z: 3, 2), (3, lambda z: z == 2, lambda z: 0, -2)]


BACKWARD_CHUNKS = (
    [(3, None, None)]
    + [
        c
        for q in range(4)
        for c in ((2, None, None), (1.5, q, None), (1.5, None, q), (1.5, None, None))
    ]
    + [(4, None, None)] + [(3.2, None, None)] * 4
    + [(1.5, 4, None), (1.5, None, 4), (3, None, None)]
    + [(1.5, 5, None), (1.5, None, 5), (5, None, None)] + [(2.6, None, None)] * 4
    + [(1.5, 6, None), (1.5, None, 6), (1.5, 7, None), (1.5, None, 7), (6, None, None)]
)


def landing_kind(order, k):
    if k == 0:
        return "s"
    axis, piece = stages_of(order)[k - 1]
    if axis == 0:
        return "z" if piece else "x"
    return "a"


def plan_backward():
    plan = Plan()
    after = {}
    done = set()
    busy = set()

    def allowed(event):
        what, u, k = event
        return what == "p" or landing_kind(SUM_ORDERS[u], k) not in busy

    def take(event, out):
        what, u, k = event
        done.add(event)
        out.append(event)
        if what == "a":
            busy.add(landing_kind(SUM_ORDERS[u], k))
            plan.time += 0.15
            plan.push(plan.time + (1.5 if k == 0 else 0.8), ("p", u, k))
            return
        busy.discard(landing_kind(SUM_ORDERS[u], k))
        plan.time += 1.5 if k == 0 else 0.5
        if k < 4:
            loads = stage_loads(SUM_ORDERS[u], k, False)
            plan.push(plan.occupy(loads), ("a", u, k + 1))

    for it in range(2):
        for i, (length, begun, sent) in enumerate(BACKWARD_CHUNKS):
            out = []
            while True:
                event = plan.pop(plan.time - SUM_MARGIN, allowed)
                if event is None:
                    break
                take(event, out)
            last = -1 if begun is None else it * 8 + begun - SLOTS
            if last >= 0:
                while ("p", last, 4) not in done:
                    take(plan.pop(1e9, allowed), out)
            plan.time += length
            if sent is not None:
                plan.push(plan.occupy([("twin", 4.0)]), ("a", it * 8 + sent, 0))
            after[it, i] = out
    rest = []
    while plan.queue:
        take(plan.pop(1e9, allowed), rest)
    return after, rest, plan.time


def backward_kernel(
    dims,
    meta,
    cot,
    w_all,
    six_in,
    xt_in,
    actt_in,
    dg_in,
    xh_in,
    rstd_in,
    lse,
    vec,
    dx_out,
    de_out,
    qkv_grad,
    out_grad,
    kv_grad,
    cq_grad,
    co_grad,
    inner_grad,
    outer_grad,
    small_out,
    cot_land,
    land_s,
    land_a,
    land_b,
    land_z,
    stage,
    ws,
    g,
    dx,
    gb,
    qkv,
    work,
    xtb,
    xh,
    rstd,
    tmp_s,
    tmp_a,
    tmp_z,
    dxb,
    deb,
    fin,
    sm,
    sm_land,
    w_sem,
    six_sem,
    xt_sem,
    dg_sem,
    xh_sem,
    cot_sem,
    cot_swap,
    s_send,
    s_recv,
    hop_send,
    hop_recv,
    tmp_sem,
    fin_sem,
    fin_send,
    fin_recv,
    out_sem,
    small_send,
    small_recv,
):
    place = Place(dims)
    core, other, at = place.core, place.other, place.at
    rank = D // (dims[0] * dims[1] * dims[2])
    place.greet()
    mine = pl.ds(core * SEQ, SEQ)
    twins = pl.ds(other * SEQ, SEQ)
    cot_send = remote(cot.at[twins], cot_land, cot_swap.at[0], cot_swap.at[1], place.twin())
    cot_send.start()
    kind = meta[1, core]

    def load_w(slot, layer, b):
        return local(w_all.at[layer * 16 + b], ws.at[slot], w_sem.at[slot])

    def load_six(slot, layer, i):
        return local(six_in.at[layer, i], qkv.at[slot], six_sem.at[slot])

    def load_xt(slot, layer, i):
        return local(xt_in.at[layer, i], xtb.at[slot], xt_sem.at[slot])

    def load_act(slot, layer, q):
        return local(actt_in.at[layer, q], xtb.at[slot], xt_sem.at[slot])

    def load_dg(slot, layer, q):
        return local(dg_in.at[layer, q], work.at[slot], dg_sem.at[slot])

    def load_xh(layer, j):
        return local(xh_in.at[layer, j], xh, xh_sem.at[0])

    def load_rstd(layer, j):
        return local(rstd_in.at[layer, j], rstd, xh_sem.at[1])

    def region(order, k, value):
        stages = stages_of(order)
        index = []
        for axis in range(3):
            if axis == stages[k][0]:
                index.append(value)
            elif axis in [a for a, _ in stages[:k]]:
                index.append(at[axis])
            else:
                index.append(slice(None))
        return tuple(index)

    def fit(order, k, pool, slot):
        free = [a for a in range(3) if isinstance(region(order, k, 0)[a], slice)]
        if pool is tmp_a and k > 0:
            return slot + ((slice(None),) if free else (0,)) + (0,)
        if pool is land_a or pool is tmp_a:
            return slot + (slice(None), pl.ds(0, dims[free[1]]))
        if pool is land_b:
            return slot + ((slice(None),) if free else (0,))
        return slot + ((pl.ds(0, dims[free[0]]),) if free else (0,))

    def pools(order, k):
        axis = stages_of(order)[k][0]
        if axis == 0:
            return land_z, tmp_z
        return (land_a if k == 0 else land_b), tmp_a

    def sends(u, k):
        order = SUM_ORDERS[u]
        axis, piece = stages_of(order)[k]
        land = pools(order, k)[0]
        found = []
        if axis != 0:
            options = [
                (step - 1, None, place.shifted(axis, step)[axis], step)
                for step in range(1, dims[axis])
            ]
        elif dims[0] == 1:
            options = []
        else:
            options = [
                (slot, test(at[0]), jnp.clip(block(at[0]), 0, dims[0] - 1), step)
                for slot, test, block, step in deep_sums(piece)
            ]
        for slot, okay, value, step in options:
            copy = remote(
                stage.at[(u % SLOTS,) + region(order, k, value)],
                land.at[fit(order, k, land, (u, slot))],
                hop_send.at[u, axis, slot],
                hop_recv.at[u, axis, slot],
                place.peer(axis, step),
            )
            found.append((okay, copy))
        return found

    def came(u, k):
        axis, piece = stages_of(SUM_ORDERS[u])[k - 1]
        if axis != 0:
            return [(step - 1, None) for step in range(1, dims[axis])]
        if dims[0] == 1:
            return []
        if piece == 0:
            return [(4, (at[0] == 1) | (at[0] == 2))]
        return [(0, at[0] >= 1), (1, at[0] <= 2), (2, at[0] >= 2), (3, at[0] <= 1)]

    def when(okay, act):
        if okay is None:
            act()
        else:
            pl.when(okay)(act)

    def arrivals(u, k):
        order = SUM_ORDERS[u]
        axis = stages_of(order)[k - 1][0]
        land, tmp = pools(order, k - 1)
        for slot, okay in came(u, k):
            spot = land.at[fit(order, k - 1, land, (u, slot))]
            wait = functools.partial(
                remote,
                spot,
                spot,
                hop_send.at[u, axis, slot],
                hop_recv.at[u, axis, slot],
                place.twin(),
            )
            load = functools.partial(
                local,
                spot,
                tmp.at[fit(order, k - 1, tmp, (slot,))],
                tmp_sem.at["sabz".index("z" if axis == 0 else ("a" if k == 1 else "b")), slot],
            )
            yield okay, wait, load

    def s_load(u):
        return local(land_s.at[u], tmp_s, tmp_sem.at[0, 0])

    def sib_send(u, parity):
        return remote(
            stage.at[SLOTS + parity], land_s.at[u], s_send.at[u], s_recv.at[u], place.twin()
        )

    def target(b):
        if b < 3:
            return qkv_grad.at[:, pl.ds(b * D, D)]
        if b < 6:
            return out_grad if b == 3 else kv_grad.at[:, pl.ds((b - 4) * D, D)]
        if b < 8:
            return cq_grad if b == 6 else co_grad
        if b < 12:
            return inner_grad.at[b - 8]
        return outer_grad.at[pl.ds((b - 12) * rank, rank)]

    def fin_local(u, side):
        turn = finals.index(u) % 2
        return local(fin.at[turn], target(PAIRS[u % 8][side]), fin_sem.at[turn])

    def fin_remote(u, side):
        turn = finals.index(u) % 2
        return remote(
            fin.at[turn], target(PAIRS[u % 8][side]), fin_send.at[u], fin_recv.at[u], place.twin()
        )

    def fin_start(u):
        layer = 1 - u // 8
        pl.when(core == layer)(lambda: fin_local(u, layer).start())
        pl.when(core != layer)(lambda: fin_remote(u, 1 - layer).start())

    def fin_wait(u):
        layer = 1 - u // 8
        pl.when(core == layer)(lambda: fin_local(u, layer).wait())
        pl.when(core != layer)(lambda: fin_remote(u, 1 - layer).wait_send())

    def add_over(slot, where, sources):
        free = [axis for axis in range(3) if isinstance(where[axis], slice)]
        total = 1
        for axis in free:
            total *= dims[axis]

        def body(i):
            found = {}
            for axis in reversed(free):
                found[axis] = lax.rem(i, dims[axis])
                i = i // dims[axis]
            index = tuple(found.get(a, where[a]) for a in range(3))
            spot = (slot,) + index
            if len(sources) == 1 and sources[0][0] is None:
                stage[spot] = stage[spot] + sources[0][1](index)
                return
            value = stage[spot].astype(FULL)
            for okay, source in sources:
                more = source(index).astype(FULL)
                value += more if okay is None else jnp.where(okay, more, 0.0)
            stage[spot] = value.astype(HALF)

        if total == 1:
            body(0)
        else:
            loop(total, body)

    def sources_of(u, k):
        order = SUM_ORDERS[u]
        tmp = pools(order, k - 1)[1]
        axis = stages_of(order)[k - 1][0]
        free = [a for a in range(3) if isinstance(region(order, k - 1, 0)[a], slice)]

        def source(slot):
            def read(index):
                if tmp is tmp_a and k > 1:
                    return tmp[slot, index[free[0]] if free else 0, 0]
                if tmp is tmp_a:
                    return tmp[slot, index[free[0]], index[free[1]]]
                return tmp[slot, index[free[0]] if free else 0]

            return read

        return [(okay, source(slot)) for slot, okay in came(u, k)]

    def sum_event(what, u, k):
        order = SUM_ORDERS[u]
        slot = u % SLOTS
        if what == "a":
            if k == 0:
                sib_send(u, u % 2).wait_recv()
                s_load(u).start()
                return
            for okay, wait, load in arrivals(u, k):

                def act(wait=wait, load=load):
                    wait().wait_recv()
                    load().start()

                when(okay, act)
            return
        if k == 0:
            axis = order[0]
            s_load(u).wait()
            sources = [(None, lambda index: tmp_s[index])]
            for (okay, copy), step in zip(sends(u, 0), range(1, dims[axis])):
                add_over(slot, region(order, 0, place.shifted(axis, step)[axis]), sources)
                copy.start()
            add_over(slot, region(order, 0, at[axis]), sources)
            return
        for okay, _, load in arrivals(u, k):
            when(okay, lambda load=load: load().wait())
        sources = sources_of(u, k)
        axis, piece = stages_of(order)[k - 1]
        if k < 4:
            if axis == 0 and piece == 0:
                if sources:
                    far = jnp.where(at[0] == 1, dims[0] - 1, 0)
                    pl.when(sources[0][0])(
                        lambda: add_over(slot, region(order, k - 1, far), [(None, sources[0][1])])
                    )
            elif sources:
                add_over(slot, region(order, k - 1, at[axis]), sources)
            for okay, copy in sends(u, k):
                when(okay, lambda copy=copy: copy.start())
            return
        turn = finals.index(u)
        if turn >= 2:
            fin_wait(finals[turn - 2])
        value = stage[(slot,) + at].astype(FULL)
        for okay, source in sources:
            more = source(at).astype(FULL)
            value += more if okay is None else jnp.where(okay, more, 0.0)
        fin[turn % 2] = value
        fin_start(u)
        for kk in range(4):
            for okay, copy in sends(u, kk):
                when(okay, lambda copy=copy: copy.wait_send())

    events, rest, _ = plan_backward()
    in_order = [e for key in sorted(events) for e in events[key]] + rest
    finals = [u for what, u, k in in_order if what == "p" and k == 4]

    chunk = D // dims[0]

    def upper(slot, h):
        return ws[slot, h].reshape(chunk, D)

    def side(it, j, which):
        return jnp.where(core == which, lax.rem(it * 8 + j, SLOTS), SLOTS + j % 2)

    def outer(index, left, right):
        for first in range(0, D, TILE):
            cols = slice(first, first + TILE)
            value = nn_dot(left[...], right[:, cols]).astype(HALF)
            stage[index, :, :, :, :, cols] = value.reshape(dims + (rank, TILE))

    def back(dst, terms, fresh, as_half=False):
        for h in range(dims[0]):
            cols = slice(h * chunk, (h + 1) * chunk)
            total = None
            for left, slot in terms:
                part = nt_dot(left[...], upper(slot, h))
                total = part if total is None else total + part
            if not fresh:
                total += dst[:, cols]
            dst[:, cols] = total.astype(HALF) if as_half else total

    def pair_free(it, j):
        if j >= 2:
            sib_send(it * 8 + j - 2, j % 2).wait_send()
        else:

            @pl.when(it > 0)
            def _():
                sib_send(it * 8 + j - 2, j % 2).wait_send()

    def emit(it, j):
        sib_send(it * 8 + j, j % 2).start()

    def norm_back(layer, j, last):
        gain = vec[layer, pl.ds(j, 1), :]
        load_xh(layer, j).wait()
        load_rstd(layer, j).wait()

        def body(i, carry):
            gains, total = carry
            rows = tile(i, ROWS)
            d = dx[rows, :]
            hat = xh[rows, :]
            dn = d * gain
            first = jnp.mean(dn, -1, keepdims=True)
            second = jnp.mean(dn * hat, -1, keepdims=True)
            out = g[rows, :] + rstd[rows, :][:, :1] * (dn - first - hat * second)
            g[rows, :] = out
            gb[rows, :] = out.astype(HALF)
            gains = gains + jnp.sum((d * hat).reshape(ROWS // 8, 8, D), 0)
            if last:
                dxb[rows, :] = out.astype(HALF)
                total = total + jnp.sum(out.reshape(ROWS // 8, 8, D), 0)
            return gains, total

        zero = jnp.zeros((8, D), FULL)
        gains, total = lax.fori_loop(0, SEQ // ROWS, body, (zero, zero))
        sm[0, layer, pl.ds(j, 1), :] = jnp.sum(gains, 0, keepdims=True)
        if last:
            whole = jnp.sum(total, 0, keepdims=True)
            sm[0, layer, pl.ds(3, 1), :] = jnp.where(kind == 1, 0.0, whole)
            sm[0, layer, pl.ds(4, 1), :] = jnp.where(kind == 1, whole, 0.0)

    def attend_back(layer, which, count, causal, point):
        def pair(hp):
            cols = tile(hp, 128)
            q2 = qkv[0, :, cols] * jnp.asarray(0.125, HALF)
            k2 = qkv[1, :, cols]
            v2 = qkv[2, :, cols]
            do2 = work[3, :, cols]
            kt = k2.T
            dk = [None, None]
            dv = [None, None]

            def put(acc, value, keys):
                for h in range(keys // TILE):
                    piece = value[h * TILE : (h + 1) * TILE]
                    acc[h] = piece if acc[h] is None else acc[h] + piece

            halves = [lane_half(0), lane_half(1)]
            ka, va, qa, da = [[m * half for half in halves] for m in (k2, v2, q2, do2)]
            keys = {f: f + TILE if causal else SEQ for f in range(0, SEQ, TILE)}
            rows = [[], []]
            for f in range(0, SEQ, TILE):
                scores, dps, probs, ds = {}, {}, {}, {}
                for a in range(2):
                    scores[a] = nt_dot(ka[a][: keys[f]], q2[f : f + TILE])
                    dps[a] = nt_dot(va[a][: keys[f]], do2[f : f + TILE])
                for a in range(2):
                    shift = lse[layer, which, hp, pl.ds(a, 1), pl.ds(f, TILE)]
                    p = jnp.exp(scores[a] - shift)
                    p = jnp.where(allowed(keys[f], f, count, causal), p, 0.0)
                    mix = jnp.sum(dps[a] * p, 0, keepdims=True)
                    ds[a] = (p * (dps[a] - mix)).astype(HALF)
                    probs[a] = p.astype(HALF)
                for a in range(2):
                    put(dv, nn_dot(probs[a], da[a][f : f + TILE]), keys[f])
                    put(dk, nn_dot(ds[a], qa[a][f : f + TILE]), keys[f])
                    rows[a].append(nn_dot(kt[a * 64 : a * 64 + 64, : keys[f]], ds[a]))
            dq = [jnp.concatenate(r, 1) for r in rows]
            whole = jnp.concatenate(dq, 0) * 0.125
            work[0, :, cols] = whole.T.astype(HALF)
            for h in range(SEQ // TILE):
                rows = pl.ds(h * TILE, TILE)
                work[1, rows, cols] = dk[h].astype(HALF)
                work[2, rows, cols] = dv[h].astype(HALF)

        for part_of in range(4):
            point()
            loop(HEADS // 8, lambda hp, part_of=part_of: pair(part_of * (HEADS // 8) + hp))

    def give(layer, src, dst, base):
        @pl.when(core == layer)
        def _():
            local(src, dst.at[mine], out_sem.at[base]).start()

        @pl.when(core != layer)
        def _():
            remote(
                src, dst.at[mine], out_sem.at[base + 1], out_sem.at[base + 2], place.twin()
            ).start()

    def given(layer, src, dst, base):
        @pl.when(core == layer)
        def _():
            local(src, dst.at[mine], out_sem.at[base]).wait()

        @pl.when(core != layer)
        def _():
            remote(
                src, dst.at[mine], out_sem.at[base + 1], out_sem.at[base + 2], place.twin()
            ).wait_send()

    def give_done(src, dst, base):
        given(0, src, dst, base)
        remote(
            src, dst.at[twins], out_sem.at[base + 1], out_sem.at[base + 2], place.twin()
        ).wait_recv()

    for slot, b in ((0, 12), (1, 8), (2, 13), (3, 9)):
        load_w(slot, 1, b).start()

    def layer_body(it):
        l = 1 - it
        passed = []

        def point():
            i = len(passed)
            passed.append(i)
            for turn in range(2):
                if events[turn, i]:

                    @pl.when(it == turn)
                    def _(turn=turn):
                        for event in events[turn, i]:
                            sum_event(*event)

        point()
        count_self = meta[0, core]
        count_cross = meta[2, core]

        @pl.when(it > 0)
        def _():
            given(1, deb, de_out, 3)

        @pl.when(core == l)
        def _():
            local(cot.at[mine], deb, cot_sem.at[0]).start()

        @pl.when(core != l)
        def _():
            remote(
                cot.at[mine], cot_land, cot_swap.at[0], cot_swap.at[1], place.twin()
            ).wait_recv()
            local(cot_land, deb, cot_sem.at[0]).start()

        for slot in range(2):
            load_dg(slot, l, slot).start()
        load_xt(0, l, 5).start()
        for q in range(2):
            load_act(1 + q, l, q).start()
        load_xt(3, l, 2).start()
        for i in range(3):
            load_six(i, l, 3 + i).start()
        load_xh(l, 2).start()
        load_rstd(l, 2).start()
        local(cot.at[mine], deb, cot_sem.at[0]).wait()

        def begin(i):
            rows = tile(i, ROWS)
            value = deb[rows, :].astype(FULL)
            value = value + jnp.where(it > 0, g[rows, :].astype(HALF).astype(FULL), 0.0)
            g[rows, :] = value
            gb[rows, :] = value.astype(HALF)

        loop(SEQ // ROWS, begin)

        for q in range(4):
            pair = 2 * (q % 2)
            point()
            load_w(pair, l, 12 + q).wait()
            load_dg(q % 2, l, q).wait()

            for h in range(dims[0]):
                cols = slice(h * chunk, (h + 1) * chunk)
                d = nt_dot(gb[...], upper(pair, h))
                work[3, :, cols] = (d * work[q % 2, :, cols].astype(FULL)).astype(HALF)
            load_act(1 + q % 2, l, q).wait()
            point()
            pair_free(it, q)
            outer(side(it, q, 0), xtb.at[1 + q % 2], gb)
            point()
            if q == 0:
                load_xt(0, l, 5).wait()
            outer(side(it, q, 1), xtb.at[0], work.at[3])
            emit(it, q)
            point()
            load_w(pair + 1, l, 8 + q).wait()
            back(dx, [(work.at[3], pair + 1)], q == 0)
            if q < 2:
                load_w(pair, l, 14 + q).start()
                load_w(pair + 1, l, 10 + q).start()
                load_dg(q, l, q + 2).start()
                load_act(1 + q, l, q + 2).start()
            elif q == 2:
                load_w(0, l, 7).start()
                load_w(1, l, 6).start()
                load_xt(1, l, 4).start()
            else:
                load_w(2, l, 4).start()
                load_w(3, l, 5).start()
                load_xt(2, l, 3).start()
                load_xt(0, l, 1).start()
        point()
        norm_back(l, 2, False)
        load_xh(l, 1).start()
        load_rstd(l, 1).start()

        load_w(0, l, 7).wait()
        back(work.at[3], [(gb, 0)], True, True)
        load_w(0, l, 3).start()
        for i in range(3):
            load_six(i, l, 3 + i).wait()
        attend_back(l, 1, count_cross, False, point)
        for i in range(3):
            load_six(i, l, i).start()
        point()
        pair_free(it, 4)
        load_xt(3, l, 2).wait()
        outer(side(it, 4, 0), xtb.at[3], work.at[1])
        point()
        outer(side(it, 4, 1), xtb.at[3], work.at[2])
        load_xt(3, l, 0).start()
        emit(it, 4)
        point()
        load_w(2, l, 4).wait()
        load_w(3, l, 5).wait()
        back(deb, [(work.at[1], 2), (work.at[2], 3)], True, True)
        load_w(2, l, 0).start()
        load_w(3, l, 1).start()
        give(l, deb, de_out, 3)
        point()
        pair_free(it, 5)
        load_xt(1, l, 4).wait()
        outer(side(it, 5, 0), xtb.at[1], gb)
        point()
        load_xt(2, l, 3).wait()
        outer(side(it, 5, 1), xtb.at[2], work.at[0])
        emit(it, 5)
        point()
        load_w(1, l, 6).wait()
        back(dx, [(work.at[0], 1)], True)
        load_w(1, l, 2).start()
        norm_back(l, 1, False)
        load_xh(l, 0).start()
        load_rstd(l, 0).start()

        load_w(0, l, 3).wait()
        back(work.at[3], [(gb, 0)], True, True)

        @pl.when(it == 0)
        def _():
            load_w(0, 0, 12).start()

        for i in range(3):
            load_six(i, l, i).wait()
        attend_back(l, 0, count_self, True, point)
        point()
        pair_free(it, 6)
        load_xt(0, l, 1).wait()
        outer(side(it, 6, 0), xtb.at[0], gb)
        point()
        load_xt(3, l, 0).wait()
        outer(side(it, 6, 1), xtb.at[3], work.at[0])
        emit(it, 6)
        point()
        pair_free(it, 7)
        outer(side(it, 7, 0), xtb.at[3], work.at[1])
        point()
        outer(side(it, 7, 1), xtb.at[3], work.at[2])
        emit(it, 7)
        point()
        load_w(1, l, 2).wait()
        load_w(2, l, 0).wait()
        load_w(3, l, 1).wait()
        back(dx, [(work.at[0], 2), (work.at[1], 3), (work.at[2], 1)], True)

        @pl.when(it == 0)
        def _():
            load_w(1, 0, 8).start()
            load_w(2, 0, 13).start()
            load_w(3, 0, 9).start()

        @pl.when(it > 0)
        def _():
            given(1, dxb, dx_out, 0)

        norm_back(l, 0, True)
        give(l, dxb, dx_out, 0)
        assert len(passed) == len(BACKWARD_CHUNKS)

    tmp_z[...] = jnp.zeros(tmp_z.shape, HALF)
    loop(2, layer_body)

    axes = (2, 1, 0)

    def small_hop(k, step, base):
        return remote(
            sm.at[k + 1],
            sm_land.at[base],
            small_send.at[base],
            small_recv.at[base],
            place.peer(axes[k], step),
        )

    def small_twin():
        return remote(sm.at[0], sm_land.at[0], small_send.at[0], small_recv.at[0], place.twin())

    def bases(k):
        first = 1
        for axis in axes[:k]:
            first += dims[axis] - 1
        return [(step, first + step - 1) for step in range(1, dims[axes[k]])]

    def small_event(k):
        if k == 0:
            small_twin().start()
            return
        if k == 1:
            small_twin().wait_recv()
            sm[1] = sm[0] + sm_land[0]
        else:
            value = sm[k - 1]
            for step, base in bases(k - 2):
                small_hop(k - 2, step, base).wait_recv()
                value += sm_land[base]
            if k == 4:
                small_out[...] = value
                return
            sm[k] = value
        for step, base in bases(k - 1):
            small_hop(k - 1, step, base).start()

    every = max(1, len(rest) // 5)
    for e in range(5):
        small_event(e)
        for event in rest[e * every : (e + 1) * every if e < 4 else None]:
            sum_event(*event)

    small_twin().wait_send()
    for k in range(3):
        for step, base in bases(k):
            small_hop(k, step, base).wait_send()
    cot_send.wait_send()
    for u in (14, 15):
        sib_send(u, u % 2).wait_send()
    for u in finals[-2:]:
        fin_wait(u)
    for layer in range(2):

        @pl.when(core == layer)
        def _(layer=layer):
            for u in range((1 - layer) * 8, (2 - layer) * 8):
                fin_remote(u, 1 - layer).wait_recv()

    give_done(dxb, dx_out, 0)
    give_done(deb, de_out, 3)


def run_backward(dims, meta, cot, w_all, saved):
    rank = D // (dims[0] * dims[1] * dims[2])
    anyw = pl.BlockSpec(memory_space=pl.ANY)
    vmem = pl.BlockSpec(memory_space=pltpu.VMEM)
    wide = max(dims[1:])
    smalls = 1 + sum(size - 1 for size in dims)
    dma = pltpu.SemaphoreType.DMA
    shape = jax.ShapeDtypeStruct
    return pl.pallas_call(
        functools.partial(backward_kernel, dims),
        out_shape=(
            shape((2 * SEQ, D), HALF),
            shape((2 * SEQ, D), HALF),
            shape((rank, 3 * D), FULL),
            shape((rank, D), FULL),
            shape((rank, 2 * D), FULL),
            shape((rank, D), FULL),
            shape((rank, D), FULL),
            shape((4, rank, D), FULL),
            shape((4 * rank, D), FULL),
            shape((2, 8, D), FULL),
            shape((SEQ, D), HALF),
            shape((16,) + dims + (rank, D), HALF),
            shape((16, wide - 1, dims[0], wide, rank, D), HALF),
            shape((16, wide - 1, dims[0], rank, D), HALF),
            shape((16, DEEP_SLOTS, wide, rank, D), HALF),
        ),
        in_specs=[pl.BlockSpec(memory_space=pltpu.SMEM)] + [anyw] * 8 + [vmem] * 2,
        out_specs=(anyw,) * 9 + (vmem,) + (anyw,) * 5,
        scratch_shapes=[
            pltpu.VMEM((SLOTS + 2,) + dims + (rank, D), HALF),
            pltpu.VMEM((4,) + dims + (rank, D), HALF),
            pltpu.VMEM((SEQ, D), FULL),
            pltpu.VMEM((SEQ, D), FULL),
            pltpu.VMEM((SEQ, D), HALF),
            pltpu.VMEM((3, SEQ, D), HALF),
            pltpu.VMEM((4, SEQ, D), HALF),
            pltpu.VMEM((4, D, SEQ), HALF),
            pltpu.VMEM((SEQ, D), FULL),
            pltpu.VMEM((SEQ, 128), FULL),
            pltpu.VMEM(dims + (rank, D), HALF),
            pltpu.VMEM((wide - 1, dims[0], wide, rank, D), HALF),
            pltpu.VMEM((DEEP_SLOTS, wide, rank, D), HALF),
            pltpu.VMEM((SEQ, D), HALF),
            pltpu.VMEM((SEQ, D), HALF),
            pltpu.VMEM((2, rank, D), FULL),
            pltpu.VMEM((4, 2, 8, D), FULL),
            pltpu.VMEM((smalls, 2, 8, D), FULL),
            dma((4,)),
            dma((3,)),
            dma((4,)),
            dma((2,)),
            dma((2,)),
            dma((1,)),
            dma((2,)),
            dma((16,)),
            dma((16,)),
            dma((16, 3, DEEP_SLOTS)),
            dma((16, 3, DEEP_SLOTS)),
            dma((4, DEEP_SLOTS)),
            dma((2,)),
            dma((16,)),
            dma((16,)),
            dma((6,)),
            dma((smalls,)),
            dma((smalls,)),
        ],
        compiler_params=pltpu.CompilerParams(
            collective_id=1, has_side_effects=True, vmem_limit_bytes=62 * 2**20
        ),
        cost_estimate=pl.CostEstimate(
            flops=80 * 10**9, bytes_accessed=4 * 10**8, transcendentals=10**7
        ),
    )(meta, cot, w_all, *saved)


def per_device(
    inputs,
    qkv_weight,
    out_weight,
    cross_query,
    cross_kv,
    cross_out,
    ffn_in,
    ffn_out,
    norm_gains,
    type_embed,
    encoder,
    lengths,
    seq_types,
    enc_mask,
    cotangent,
):
    chips = lax.axis_size("dp")
    dims = grid_of(chips)
    rank = D // chips
    pack = packed(
        qkv_weight, out_weight, cross_query, cross_kv, cross_out, ffn_in, ffn_out, chips
    )
    small = small_block(norm_gains, type_embed)
    meta = jnp.stack([lengths, seq_types, jnp.sum(enc_mask, 1)])
    w_all, outs, *saved = run_forward(dims, meta, pack, small, inputs, encoder[0])
    grads = run_backward(dims, meta, cotangent[0], w_all, saved)
    d_in, d_mem, d_qkv, d_out, d_kv, d_cq, d_co, inner, outer, sums = grads[:10]

    inner = inner.reshape(4, rank, chips, rank).transpose(1, 2, 0, 3)
    own = lax.dynamic_index_in_dim(sums, lax.axis_index("section"), 0, keepdims=False)
    own = lax.dynamic_slice_in_dim(own, lax.axis_index("dp") * rank, rank, 1)
    return (
        outs[None],
        d_in[None],
        d_mem[None],
        d_qkv[None],
        d_out[None],
        d_cq[None],
        d_kv[None],
        d_co[None],
        inner.reshape(1, rank, 4 * D),
        outer[None],
        own[None, :3],
        own[None, 3:5],
    )


def solution(mesh):
    rows = P("section", "dp", None)
    cols = P("section", None, "dp")
    in_specs = (
        (P("dp", None),)
        + (rows,) * 7
        + (cols, cols, rows, P("dp"), P("dp"), P("dp", None), rows)
    )
    out_specs = (rows,) * 10 + (cols, cols)
    return jax.shard_map(
        per_device, mesh=mesh, in_specs=in_specs, out_specs=out_specs, check_vma=False
    )
```
